128 devices in a mesh: fsdp: 16 (over x_lo, z, core), tp: 8 (over y, x_hi).
Axes of the slice: x: 4 (x_hi: 2, x_lo: 2; x = x_hi * 2 + x_lo), y: 4, z: 4, core: 2. Of those that a mesh axis runs over, the one named last changes fastest.
Arguments:
- attn_out: bfloat16 [16384, 8192], P('fsdp', 'tp'), may hold values from -6 to 6
- out_grad: bfloat16 [16384, 5120], P('fsdp'), may hold values from -6 to 6
- master: float32 [5120, 8192], P('fsdp', 'tp'), may hold values from -0.0625 to 0.0625
- moment_one: float32 [5120, 8192], P('fsdp', 'tp'), may hold values from -0.15625 to 0.15625
- moment_two: float32 [5120, 8192], P('fsdp', 'tp'), may hold values from 1e-05 to 0.001
- query: bfloat16 [128, 8192], P('fsdp', 'tp'), may hold values from -150 to 150
- incoming_key: bfloat16 [128, 1024], P('fsdp', 'tp'), may hold values from -6 to 6
- incoming_value: bfloat16 [128, 1024], P('fsdp', 'tp'), may hold values from -48 to 48
- key_cache: bfloat16 [128, 8, 1024, 128], P('fsdp', 'tp'), may hold values from -6 to 6
- stored_value_cache: bfloat16 [128, 8, 1024, 128], P('fsdp', 'tp'), may hold values from -48 to 48
- cache_lengths: int32 [128], P('fsdp'), may hold values from 256 to 1024, as said below
Outputs:
- master_new: float32 [5120, 8192], P('fsdp', 'tp')
- moment_one_new: float32 [5120, 8192], P('fsdp', 'tp')
- moment_two_new: float32 [5120, 8192], P('fsdp', 'tp')
- decoded: bfloat16 [128, 5120], P('fsdp', 'tp')
The draws below stay inside these ranges and needn't reach their ends.
Inputs may be any that keep to these rules, and one draw needn't show every extreme that they name: `cache_lengths`: some row has exactly 1024 filled slots.
All inputs are finite; a program needn't handle non-finite values.
Results may differ from the reference program's by a relative error of at most 0.022.
Values may be sent and summed in bfloat16 or wider, within the bound.
A program may use at most 128 MiB of HBM per device.

```python
import math
import jax
import jax.numpy as jnp
from jax import lax

D = 5120
QUERY_HEADS = 64
KEY_VALUE_HEADS = 8
HEAD_SIZE = 128
TOK_DEV = 1024
CACHE_SLOTS = 1024
HQD = 8192
TOKENS = 16384
DECODE_ROW_TOTAL = 128
N_FSDP = 16


def cache_keys(key):
    return jnp.clip(jax.random.normal(key, (DECODE_ROW_TOTAL, KEY_VALUE_HEADS, CACHE_SLOTS, HEAD_SIZE), jnp.float32), -6.0, 6.0)


def draw_key_cache(key, part):
    base = cache_keys(key)
    return base.astype(jnp.bfloat16)


def draw_query(key, part):
    key = jax.random.fold_in(key, 5)
    first = jax.random.fold_in(key, 0)
    values = jnp.clip(jax.random.normal(first, (DECODE_ROW_TOTAL, QUERY_HEADS * HEAD_SIZE), jnp.float32), -6.0, 6.0)
    return values.astype(jnp.bfloat16)


def draw_cache_lengths(key, part):
    key = jax.random.fold_in(key, 11)
    first, second = jax.random.split(key)
    lengths = jax.random.randint(first, (DECODE_ROW_TOTAL,), CACHE_SLOTS // 4, CACHE_SLOTS + 1)
    longest = jax.random.randint(second, (), 0, DECODE_ROW_TOTAL)
    return lengths.at[longest].set(CACHE_SLOTS).astype(jnp.int32)


def block_scale(key, dims, pieces, least, high):
    gain = 1.0
    for dim, blocks in pieces:
        heights = jax.random.uniform(jax.random.fold_in(jax.random.fold_in(key, 6), dim), (blocks,), jnp.float32, least / len(pieces), high / len(pieces))
        gain = gain * jnp.repeat(jnp.exp(heights), dims[dim] // blocks).reshape((-1,) + (1,) * (len(dims) - 1 - dim))
    return gain


def normal_values(rng, dims, deviation, limit, cuts=(), held_as=jnp.bfloat16):
    result = jax.random.normal(rng, dims, jnp.float32) * deviation
    if len(cuts) > 0:
        result = block_scale(rng, dims, cuts, -0.22, 0.18) * result
    return jnp.clip(result, min=-limit, max=limit).astype(held_as)


def setup_inputs(seed: int = 0) -> dict:
    key_of = jax.random.split(jax.random.key(seed), 12)
    attn_out = normal_values(key_of[0], (TOKENS, HQD), 1.0, 6.0, ((0, 16), (1, 8)))
    out_grad = normal_values(key_of[1], (TOKENS, D), 1.0, 6.0, ((0, 16),))
    master = normal_values(key_of[2], (D, HQD), HQD ** -0.5, 0.0625, ((0, 16), (1, 8)), jnp.float32)
    moment_one = normal_values(key_of[3], (D, HQD), 0.01, 0.15625, ((0, 16), (1, 8)), jnp.float32)
    moment_two = jnp.clip(jnp.exp(math.log(0.001) - 4.6051703 * jax.random.uniform(key_of[4], (D, HQD), jnp.float32) ** block_scale(key_of[4], (D, HQD), ((0, 16), (1, 8)), -0.2, 0.2)), 9.999999747378752e-06, 0.001)
    query = draw_query(jax.random.fold_in(key_of[11], 71), 0)
    incoming_key = normal_values(key_of[6], (DECODE_ROW_TOTAL, KEY_VALUE_HEADS * HEAD_SIZE), 1.0, 6.0, ((0, 16), (1, 8)))
    incoming_value = normal_values(key_of[7], (DECODE_ROW_TOTAL, KEY_VALUE_HEADS * HEAD_SIZE), 8.0, 48.0, ((0, 16), (1, 8)))
    key_cache = draw_key_cache(jax.random.fold_in(key_of[11], 71), 0)
    stored_value_cache = normal_values(key_of[9], (DECODE_ROW_TOTAL, KEY_VALUE_HEADS, CACHE_SLOTS, HEAD_SIZE), 8.0, 48.0, ((0, 16), (1, 8)))
    cache_lengths = draw_cache_lengths(jax.random.fold_in(key_of[11], 71), 0)
    return {"attn_out": attn_out, "out_grad": out_grad, "master": master, "moment_one": moment_one, "moment_two": moment_two, "query": query, "incoming_key": incoming_key, "incoming_value": incoming_value, "key_cache": key_cache, "stored_value_cache": stored_value_cache, "cache_lengths": cache_lengths}


beta_one = 0.9
beta_two = 0.95
learn_rate = 0.003
weight_decay = 0.1
adam_eps = 1e-08
bias_one = 1.0 - 0.9 ** 10
bias_two = 1.0 - 0.95 ** 10

def reference(attn_out, out_grad, master, moment_one, moment_two, query, incoming_key, incoming_value, key_cache, stored_value_cache, cache_lengths):
    blocks_attn = attn_out.reshape(N_FSDP, TOK_DEV, HQD)
    blocks_grad = out_grad.reshape(N_FSDP, TOK_DEV, D)

    def accumulate(total, pair):
        grad_block, attn_block = pair
        term = lax.dot_general(grad_block, attn_block, (((0,), (0,)), ((), ())), preferred_element_type=jnp.float32)
        rounded = lax.optimization_barrier(term.astype(jnp.bfloat16))
        return (total + rounded.astype(jnp.float32), None)
    summed, _ = lax.scan(accumulate, jnp.zeros((D, HQD), jnp.float32), (blocks_grad, blocks_attn))
    grad = summed / TOKENS
    moment_one_new = beta_one * moment_one + (1.0 - beta_one) * grad
    moment_two_new = beta_two * moment_two + (1.0 - beta_two) * grad * grad
    update = moment_one_new / bias_one / (jnp.sqrt(moment_two_new / bias_two) + adam_eps)
    master_new = master * (1.0 - learn_rate * weight_decay) - learn_rate * update
    weights = master_new.astype(jnp.bfloat16)
    group_index = QUERY_HEADS // KEY_VALUE_HEADS
    score_scale = 1.0 / HEAD_SIZE ** 0.5
    slots = jnp.arange(CACHE_SLOTS, dtype=jnp.int32)

    def decode_row(items):
        current_row_query, current_row_key, current_row_value, row_kcache, row_vcache, row_length = items
        query_rows = current_row_query.astype(jnp.float32).reshape(KEY_VALUE_HEADS, group_index, HEAD_SIZE)
        cached = jnp.einsum('gqd,gcd->gqc', query_rows, row_kcache.astype(jnp.float32)) * score_scale
        cached = jnp.where((slots < row_length)[None, None, :], cached, -jnp.inf)
        fresh_scores = jnp.einsum('jvs,js->jv', query_rows, current_row_key.astype(jnp.float32).reshape(KEY_VALUE_HEADS, HEAD_SIZE)) * score_scale
        top = jnp.maximum(lax.optimization_barrier(jnp.max(cached, axis=-1)), fresh_scores)
        expo_cached = jnp.exp(cached - top[..., None])
        expo_fresh = jnp.exp(fresh_scores - top)
        total = lax.optimization_barrier(jnp.sum(expo_cached, axis=-1)) + expo_fresh
        probs = (expo_cached / total[..., None]).astype(jnp.bfloat16)
        fresh_probabilities = (expo_fresh / total).astype(jnp.bfloat16)
        mixed_output = jnp.einsum('gqc,gcd->gqd', probs.astype(jnp.float32), row_vcache.astype(jnp.float32))
        mixed_output = mixed_output + fresh_probabilities.astype(jnp.float32)[..., None] * current_row_value.astype(jnp.float32).reshape(KEY_VALUE_HEADS, 1, HEAD_SIZE)
        return mixed_output.reshape(HQD).astype(jnp.bfloat16)
    attended = lax.map(decode_row, (query, incoming_key, incoming_value, key_cache, stored_value_cache, cache_lengths))
    decoded = lax.dot_general(attended, weights, (((1,), (1,)), ((), ())), preferred_element_type=jnp.float32)
    return (master_new, moment_one_new, moment_two_new, decoded.astype(jnp.bfloat16))
```

```python
import functools

import jax
import jax.numpy as jnp
from jax import lax
from jax.experimental import pallas as pl
from jax.experimental.pallas import tpu as pltpu
from jax.sharding import PartitionSpec as P

MESH = pl.DeviceIdType.MESH
HEAD_SIZE = 128
CACHE_SLOTS = 1024
TOKENS = 16384

beta_one = 0.9
beta_two = 0.95
learn_rate = 0.003
weight_decay = 0.1
adam_eps = 1e-08
bias_one = 1.0 - 0.9**10
bias_two = 1.0 - 0.95**10

NX, NZ = 2, 4
ROWS = 320
COLS = 1024
X_ROWS = 144
Z_ROWS = ROWS - X_ROWS
ORDER = ((1, 2), (1, 1), (1, 3), (0, 2), (0, 1), (0, 3), (1, 0), (0, 0))
SLOT = {place: slot for slot, place in enumerate(ORDER)}
STREAMS = {"zo": (X_ROWS, Z_ROWS, 96), "zs": (X_ROWS, Z_ROWS, 96), "x": (0, X_ROWS, 64)}


def kernel(
    attn_hbm,
    grad_hbm,
    master_hbm,
    one_hbm,
    two_hbm,
    query_hbm,
    new_key_hbm,
    new_value_hbm,
    keys_hbm,
    values_hbm,
    lengths,
    master_out,
    one_out,
    two_out,
    decoded_ref,
    attn,
    grads,
    part,
    from_core,
    from_x,
    from_x_last,
    zo_near,
    zo_far,
    zs_near,
    zs_far,
    x_near,
    x_far,
    master,
    one,
    two,
    query,
    new_key,
    new_value,
    keys,
    values,
    weights,
    heads,
    mixed,
    fresh,
    attended,
    shares,
    arrived,
    load_sem,
    grad_sem,
    core_sem,
    x_sem,
    z_sem,
    attend_sem,
    share_send,
    share_recv,
    store_sem,
):
    f = lax.axis_index("fsdp")
    t = lax.axis_index("tp")
    x, z, k = f // (2 * NZ), lax.rem(f // 2, NZ), lax.rem(f, 2)

    def at(dx, dz, core):
        return ((lax.rem(x + dx, NX) * NZ + lax.rem(z + dz, NZ)) * 2 + core, t)

    def chip(dx, dz):
        return lax.rem(x + dx, NX) * NZ + lax.rem(z + dz, NZ)

    other_core = at(0, 0, 1 - k)
    other_x = at(1, 0, k)
    up, down = at(0, 1, k), at(0, 3, k)
    own = pl.multiple_of(k * ROWS, 64)
    given = pl.multiple_of((1 - k) * ROWS, 64)

    def load(src, dst, n):
        return pltpu.make_async_copy(src, dst, load_sem.at[n])

    attn_load = load(attn_hbm, attn, 0)
    grad_loads = []
    for slot, (dx, dz) in enumerate(ORDER):
        columns = pl.ds(pl.multiple_of(chip(dx, dz) * 2 * ROWS, 128), 2 * ROWS)
        grad_loads.append(
            pltpu.make_async_copy(grad_hbm.at[:, columns], grads.at[slot], grad_sem.at[slot])
        )
    late_loads = [
        load(src, dst, n + 1)
        for n, (src, dst) in enumerate(
            (
                (query_hbm, query),
                (new_key_hbm, new_key),
                (new_value_hbm, new_value),
                (keys_hbm, keys),
                (values_hbm, values),
                (master_hbm, master),
                (one_hbm, one),
                (two_hbm, two),
            )
        )
    ]
    grad_loads[0].start()
    attn_load.start()
    for copy in grad_loads[1:]:
        copy.start()

    barrier = pltpu.get_barrier_semaphore()

    def greet(device):
        pl.semaphore_signal(barrier, inc=1, device_id=device, device_id_type=MESH)

    greet(other_core)
    for place in range(1, NX * NZ):
        greet(at(place // NZ, place % NZ, k))
    self_share = t == f // 2
    for core in range(2):
        for step in range(8):
            source = (2 * t + core, lax.rem(t + step, 8))
            if step == 0:
                @pl.when(jnp.logical_not(jnp.logical_and(self_share, k == core)))
                def _():
                    greet(source)
            else:
                greet(source)
    for copy in late_loads:
        copy.start()

    def remote(src, dst, send, recv, device):
        return pltpu.make_async_remote_copy(
            src_ref=src, dst_ref=dst, send_sem=send, recv_sem=recv, device_id=device, device_id_type=MESH
        )

    def core_copy(slot):
        return remote(
            part.at[slot, pl.ds(given, ROWS)],
            from_core.at[slot],
            core_sem.at[0, slot],
            core_sem.at[1, slot],
            other_core,
        )

    def rows_of(dx, dz, first, count):
        return part.at[SLOT[dx, dz], pl.ds(pl.multiple_of(own + first, 16), count)]

    def add(dst_ref, slot, first, src_ref, src_first, count):
        @pl.loop(0, count // 16)
        def _(n):
            rows = pl.ds(pl.multiple_of(first + n * 16, 16), 16)
            dst_ref[slot, rows, :] = (
                dst_ref[slot, rows, :] + src_ref[pl.ds(pl.multiple_of(src_first + n * 16, 16), 16), :]
            )

    def add_own(dx, dz, first, src_ref, src_first, count):
        add(part, SLOT[dx, dz], own + first, src_ref, src_first, count)

    over_x = [
        remote(rows_of(1, dz, 0, X_ROWS), from_x.at[dz], x_sem.at[0, dz], x_sem.at[1, dz], other_x)
        for dz in range(NZ)
    ]
    last_x = remote(
        rows_of(1, 0, X_ROWS, Z_ROWS), from_x_last, x_sem.at[0, NZ], x_sem.at[1, NZ], other_x
    )

    class Stream:
        def __init__(self, number, name, dx, near, far):
            first, count, cut = STREAMS[name]
            self.first, self.count, self.cut = first, count, cut
            self.dx, self.near, self.far = dx, near, far

            def send(dz, begin, size, dst, n, device):
                return remote(
                    rows_of(dx, dz, first + begin, size),
                    dst,
                    z_sem.at[0, number, n],
                    z_sem.at[1, number, n],
                    device,
                )

            rest = count - cut
            self.far_up = send(2, 0, cut, far.at[pl.ds(0, cut)], 0, up)
            self.far_down = send(2, cut, rest, far.at[pl.ds(cut, rest)], 1, down)
            self.up_free = send(1, cut, rest, near.at[0, pl.ds(cut, rest)], 2, up)
            self.up_late = send(1, 0, cut, near.at[0, pl.ds(0, cut)], 3, up)
            self.down_free = send(3, 0, cut, near.at[1, pl.ds(0, cut)], 4, down)
            self.down_late = send(3, cut, rest, near.at[1, pl.ds(cut, rest)], 5, down)
            self.copies = (
                self.far_up, self.far_down, self.up_free, self.up_late, self.down_free, self.down_late
            )

        def start_far(self):
            self.far_up.start()
            self.far_down.start()

        def pass_far_up(self):
            self.far_up.wait_recv()
            add_own(self.dx, 1, self.first, self.far, 0, self.cut)
            self.up_late.start()

        def pass_far_down(self):
            self.far_down.wait_recv()
            add_own(self.dx, 3, self.first + self.cut, self.far, self.cut, self.count - self.cut)
            self.down_late.start()

        def wait_near(self):
            for copy in self.copies[2:]:
                copy.wait_recv()

        def add_near(self):
            self.wait_near()
            for side in range(2):
                add_own(self.dx, 0, self.first, self.near.at[side], 0, self.count)

    zo = Stream(0, "zo", 1, zo_near, zo_far)
    zs = Stream(1, "zs", 0, zs_near, zs_far)
    xs = Stream(2, "x", 0, x_near, x_far)

    def after_slab(slot):
        dx, dz = ORDER[slot]
        if dx == 1:
            over_x[dz].start()
        stream = zo if dx == 1 else zs
        if dz == 2:
            stream.start_far()
        if dz == 1:
            stream.up_free.start()
        if dz == 3:
            stream.down_free.start()

    def x_far():
        over_x[2].wait_recv()
        add_own(0, 2, 0, from_x.at[2], 0, X_ROWS)
        xs.start_far()

    attn_load.wait()

    @pl.loop(0, len(ORDER) + 1)
    def _(step):
        @pl.when(step < len(ORDER))
        def _():
            pltpu.make_async_copy(
                grad_hbm.at[:, pl.ds(0, 2 * ROWS)], grads.at[step], grad_sem.at[step]
            ).wait()
            part[step] = lax.dot_general(
                grads[step], attn[...], (((0,), (0,)), ((), ())), preferred_element_type=jnp.float32
            ).astype(jnp.bfloat16)

        @pl.when(step == 0)
        def _():
            pl.semaphore_wait(barrier, 8 + 16 - self_share.astype(jnp.int32))

        @pl.when(step < len(ORDER))
        def _():
            core_copy(step).start()

        @pl.when(step > 0)
        def _():
            core_copy(step - 1).wait_recv()
            add(part, step - 1, own, from_core.at[step - 1], 0, ROWS)

        for slot in range(len(ORDER)):
            @pl.when(step == slot + 1)
            def _():
                after_slab(slot)
                if slot == 5:
                    zo.pass_far_up()
                    zo.pass_far_down()
                if slot == 6:
                    x_far()

    for copy in late_loads:
        copy.wait()
    for head in range(8):
        heads[pl.ds(8 * head, 8), :] = query[:, pl.ds(HEAD_SIZE * head, HEAD_SIZE)].astype(jnp.float32)
    fresh[0] = new_key[...].astype(jnp.float32)
    fresh[1] = new_value[...].astype(jnp.float32)
    score_scale = 1.0 / HEAD_SIZE**0.5

    def attend(row):
        own_heads = heads[pl.ds(row, 8, stride=8), :]
        scores = (
            lax.dot_general(
                own_heads.astype(jnp.bfloat16),
                keys[row, 0],
                (((1,), (1,)), ((), ())),
                preferred_element_type=jnp.float32,
            )
            * score_scale
        )
        slots = lax.broadcasted_iota(jnp.int32, (8, CACHE_SLOTS), 1)
        scores = jnp.where(slots < lengths[row], scores, -jnp.inf)
        new_score = (
            jnp.sum(own_heads * fresh[0, pl.ds(row, 1), :], axis=-1, keepdims=True) * score_scale
        )
        top = jnp.maximum(jnp.max(scores, axis=-1, keepdims=True), new_score)
        expo = jnp.exp(scores - top)
        expo_new = jnp.exp(new_score - top)
        total = jnp.sum(expo, axis=-1, keepdims=True) + expo_new
        probs = (expo / total).astype(jnp.bfloat16)
        prob_new = (expo_new / total).astype(jnp.bfloat16).astype(jnp.float32)
        mixed[pl.ds(row, 8, stride=8), :] = (
            jnp.dot(probs, values[row, 0], preferred_element_type=jnp.float32)
            + prob_new * fresh[1, pl.ds(row, 1), :]
        )

    @pl.loop(0, 4)
    def _(row):
        attend(row)

    zo.add_near()
    last_x.start()

    @pl.loop(4, 8)
    def _(row):
        attend(row)

    halves = [
        jnp.concatenate([mixed[pl.ds(8 * head, 8), :] for head in range(4 * half, 4 * half + 4)], axis=1)
        for half in range(2)
    ]
    here = chip(0, 0)
    attended[k, here] = jnp.concatenate(halves, axis=0).astype(jnp.bfloat16)
    gathers = [
        remote(
            attended.at[k, here],
            attended.at[k, here],
            attend_sem.at[0, place],
            attend_sem.at[1, place],
            at(place // NZ, place % NZ, k),
        )
        for place in range(1, NX * NZ)
    ]
    for copy in gathers:
        copy.start()

    over_x[1].wait_recv()
    add_own(0, 1, 0, from_x.at[1], 0, X_ROWS)
    xs.up_free.start()
    zs.pass_far_up()
    zs.pass_far_down()
    xs.pass_far_up()
    over_x[3].wait_recv()
    add_own(0, 3, 0, from_x.at[3], 0, X_ROWS)
    xs.down_free.start()
    xs.pass_far_down()

    for copy in gathers:
        copy.wait_recv()
    swap = remote(
        attended.at[k], attended.at[k], attend_sem.at[0, 0], attend_sem.at[1, 0], other_core
    )
    swap.start()

    def adam(first, count, terms):
        slot = SLOT[0, 0]

        @pl.loop(0, count // 16)
        def _(n):
            begin = pl.multiple_of(n * 16, 16)
            rows = pl.ds(pl.multiple_of(first + begin, 16), 16)
            total = part[slot, pl.ds(pl.multiple_of(own + first + begin, 16), 16), :].astype(jnp.float32)
            for term in terms:
                total = total + term[pl.ds(begin, 16), :].astype(jnp.float32)
            grad = total * (1.0 / TOKENS)
            one_new = beta_one * one[rows, :] + (1.0 - beta_one) * grad
            two_new = beta_two * two[rows, :] + (1.0 - beta_two) * grad * grad
            update = one_new / bias_one / (jnp.sqrt(two_new / bias_two) + adam_eps)
            master_new = master[rows, :] * (1.0 - learn_rate * weight_decay) - learn_rate * update
            one[rows, :] = one_new
            two[rows, :] = two_new
            master[rows, :] = master_new
            weights[rows, :] = master_new.astype(jnp.bfloat16)

    zs.wait_near()
    over_x[0].wait_recv()
    last_x.wait_recv()
    adam(X_ROWS, Z_ROWS, (from_x_last, zs_near.at[0], zs_near.at[1]))
    xs.wait_near()
    adam(0, X_ROWS, (from_x.at[0], x_near.at[0], x_near.at[1]))
    stores = [
        pltpu.make_async_copy(src, dst, store_sem.at[n])
        for n, (src, dst) in enumerate(((master, master_out), (one, one_out), (two, two_out)))
    ]
    for copy in stores:
        copy.start()

    swap.wait_recv()
    every = attended[...].reshape(256, 512)
    products = [
        lax.dot_general(
            every,
            weights[:, pl.ds(512 * half, 512)],
            (((1,), (1,)), ((), ())),
            preferred_element_type=jnp.float32,
        ).reshape(2, 8, 16, ROWS)[:, :, 8 * half : 8 * half + 8, :]
        for half in range(2)
    ]
    shares[...] = products[0] + products[1]

    def share_copy(step):
        target = lax.rem(f + step, 16)
        return remote(
            shares.at[lax.rem(target, 2), target // 2],
            arrived.at[k, t],
            share_send.at[step],
            share_recv.at[k, t],
            (target, f // 2),
        )

    @pl.when(self_share)
    def _():
        pltpu.make_async_copy(shares.at[k, f // 2], arrived.at[k, t], share_recv.at[k, t]).start()

    @pl.when(jnp.logical_not(self_share))
    def _():
        share_copy(0).start()

    for step in range(1, 16):
        share_copy(step).start()
    for core in range(2):
        for group in range(8):
            pltpu.make_async_copy(
                shares.at[0, 0], arrived.at[core, group], share_recv.at[core, group]
            ).wait()
    decoded_ref[...] = jnp.concatenate(
        [jnp.sum(arrived[core], axis=0) for core in range(2)], axis=1
    )

    @pl.when(jnp.logical_not(self_share))
    def _():
        share_copy(0).wait_send()

    for step in range(1, 16):
        share_copy(step).wait_send()
    for slot in range(len(ORDER)):
        core_copy(slot).wait_send()
    for copy in (*over_x, last_x, *zo.copies, *zs.copies, *xs.copies, *gathers, swap):
        copy.wait_send()
    for copy in stores:
        copy.wait()


def shards(*args):
    any_space = pl.BlockSpec(memory_space=pl.ANY)
    bf16, f32 = jnp.bfloat16, jnp.float32
    results = pl.pallas_call(
        kernel,
        out_shape=(
            jax.ShapeDtypeStruct((ROWS, COLS), f32),
            jax.ShapeDtypeStruct((ROWS, COLS), f32),
            jax.ShapeDtypeStruct((ROWS, COLS), f32),
            jax.ShapeDtypeStruct((8, 640), f32),
        ),
        in_specs=[any_space] * 10 + [pl.BlockSpec(memory_space=pltpu.SMEM)],
        out_specs=(any_space,) * 3 + (pl.BlockSpec(memory_space=pltpu.VMEM),),
        scratch_shapes=[
            pltpu.VMEM((1024, COLS), bf16),
            pltpu.VMEM((8, 1024, 2 * ROWS), bf16),
            pltpu.VMEM((8, 2 * ROWS, COLS), bf16),
            pltpu.VMEM((8, ROWS, COLS), bf16),
            pltpu.VMEM((NZ, X_ROWS, COLS), bf16),
            pltpu.VMEM((Z_ROWS, COLS), bf16),
            pltpu.VMEM((2, Z_ROWS, COLS), bf16),
            pltpu.VMEM((Z_ROWS, COLS), bf16),
            pltpu.VMEM((2, Z_ROWS, COLS), bf16),
            pltpu.VMEM((Z_ROWS, COLS), bf16),
            pltpu.VMEM((2, X_ROWS, COLS), bf16),
            pltpu.VMEM((X_ROWS, COLS), bf16),
            pltpu.VMEM((ROWS, COLS), f32),
            pltpu.VMEM((ROWS, COLS), f32),
            pltpu.VMEM((ROWS, COLS), f32),
            pltpu.VMEM((8, 1024), bf16),
            pltpu.VMEM((8, HEAD_SIZE), bf16),
            pltpu.VMEM((8, HEAD_SIZE), bf16),
            pltpu.VMEM((8, 1, CACHE_SLOTS, HEAD_SIZE), bf16),
            pltpu.VMEM((8, 1, CACHE_SLOTS, HEAD_SIZE), bf16),
            pltpu.VMEM((ROWS, COLS), bf16),
            pltpu.VMEM((64, HEAD_SIZE), f32),
            pltpu.VMEM((64, HEAD_SIZE), f32),
            pltpu.VMEM((2, 8, HEAD_SIZE), f32),
            pltpu.VMEM((2, 8, 16, 512), bf16),
            pltpu.VMEM((2, 8, 8, ROWS), f32),
            pltpu.VMEM((2, 8, 8, ROWS), f32),
            pltpu.SemaphoreType.DMA((9,)),
            pltpu.SemaphoreType.DMA((8,)),
            pltpu.SemaphoreType.DMA((2, 8)),
            pltpu.SemaphoreType.DMA((2, NZ + 1)),
            pltpu.SemaphoreType.DMA((2, 3, 6)),
            pltpu.SemaphoreType.DMA((2, 8)),
            pltpu.SemaphoreType.DMA((16,)),
            pltpu.SemaphoreType.DMA((2, 8)),
            pltpu.SemaphoreType.DMA((3,)),
        ],
        compiler_params=pltpu.CompilerParams(
            collective_id=0, has_side_effects=True, vmem_limit_bytes=58 << 20
        ),
        cost_estimate=pl.CostEstimate(
            flops=2 * 1024 * 1024 * 5120, bytes_accessed=24 << 20, transcendentals=1 << 19
        ),
    )(*args)
    return (*results[:3], results[3].astype(jnp.bfloat16))


def solution(mesh):
    placed = (
        P("fsdp", "tp"),
        P("fsdp", None),
        P("fsdp", "tp"),
        P("fsdp", "tp"),
        P("fsdp", "tp"),
        P("fsdp", "tp"),
        P("fsdp", "tp"),
        P("fsdp", "tp"),
        P("fsdp", "tp", None, None),
        P("fsdp", "tp", None, None),
        P("fsdp"),
    )
    return jax.shard_map(
        shards,
        mesh=mesh,
        in_specs=placed,
        out_specs=(P("fsdp", "tp"), P("fsdp", "tp"), P("fsdp", "tp"), P("fsdp", "tp")),
        check_vma=False,
    )
```

```python
import jax
import jax.numpy as jnp
from jax import lax
from jax.experimental import pallas as pl
from jax.experimental.pallas import tpu as pltpu
from jax.sharding import PartitionSpec as P

MESH = pl.DeviceIdType.MESH
HEAD_SIZE = 128
CACHE_SLOTS = 1024
TOKENS = 16384

beta_one = 0.9
beta_two = 0.95
learn_rate = 0.003
weight_decay = 0.1
adam_eps = 1e-08
bias_one = 1.0 - 0.9**10
bias_two = 1.0 - 0.95**10

NX, NZ = 2, 4
ROWS = 320
COLS = 1024
HALF = COLS // 2
X_ROWS = 144
Z_ROWS = ROWS - X_ROWS
PADDED = 384
ORDER = ((1, 2), (1, 1), (1, 3), (0, 2), (0, 1), (0, 3), (1, 0), (0, 0))
SLABS = len(ORDER)
STEPS = 2 * SLABS
SLOT = {place: slot for slot, place in enumerate(ORDER)}
STREAMS = ((1, X_ROWS, Z_ROWS, 96), (0, X_ROWS, Z_ROWS, 96), (0, 0, X_ROWS, 64))


def kernel(
    attn_hbm,
    grad_hbm,
    master_hbm,
    one_hbm,
    two_hbm,
    query_hbm,
    new_key_hbm,
    new_value_hbm,
    keys_hbm,
    values_hbm,
    lengths_hbm,
    master_out,
    one_out,
    two_out,
    decoded_out,
    attn,
    grads,
    part,
    from_core,
    from_x,
    from_x_last,
    zo_near,
    zo_far,
    zs_near,
    zs_far,
    xs_near,
    xs_far,
    master,
    one,
    two,
    query,
    new_key,
    new_value,
    keys,
    values,
    lengths,
    weights,
    heads,
    mixed,
    fresh,
    attended,
    shares,
    arrived,
    totals,
    decoded,
    load_sem,
    attn_sem,
    grad_sem,
    core_sem,
    x_sem,
    z_sem,
    attend_sem,
    share_sem,
    send_sem,
):
    f = lax.axis_index("fsdp")
    t = lax.axis_index("tp")
    x, z, k = f // (2 * NZ), lax.rem(f // 2, NZ), lax.rem(f, 2)
    y, x_hi = t // 2, lax.rem(t, 2)
    z_summed = lax.rem(z + 2 + y - f // 4 + 8, NZ)

    def chip(dx, dz):
        return lax.rem(x + dx, NX) * NZ + lax.rem(z + dz, NZ)

    def at(dx, dz, core):
        return (chip(dx, dz) * 2 + core, t)

    other_core = at(0, 0, 1 - k)
    other_x = at(1, 0, k)
    up, down = at(0, 1, k), at(0, 3, k)
    own = pl.multiple_of(k * ROWS, 64)
    given = pl.multiple_of((1 - k) * ROWS, 64)

    attn_loads = [
        pltpu.make_async_copy(attn_hbm.at[:, pl.ds(HALF * half, HALF)], attn.at[half], attn_sem.at[half])
        for half in range(2)
    ]
    grad_loads = []
    for slot, (dx, dz) in enumerate(ORDER):
        columns = pl.ds(pl.multiple_of(chip(dx, dz) * 2 * ROWS, 128), 2 * ROWS)
        grad_loads.append(
            pltpu.make_async_copy(grad_hbm.at[:, columns], grads.at[slot], grad_sem.at[slot])
        )
    late_loads = [
        pltpu.make_async_copy(src, dst, load_sem.at[n])
        for n, (src, dst) in enumerate(
            (
                (query_hbm, query),
                (new_key_hbm, new_key),
                (new_value_hbm, new_value),
                (lengths_hbm, lengths),
                (keys_hbm, keys),
                (values_hbm, values),
                (master_hbm, master),
                (one_hbm, one),
                (two_hbm, two),
            )
        )
    ]
    grad_loads[0].start()
    attn_loads[0].start()

    barrier = pltpu.get_barrier_semaphore()

    def greet(device):
        pl.semaphore_signal(barrier, inc=1, device_id=device, device_id_type=MESH)

    greet(other_core)
    for place in range(1, NX * NZ):
        greet(at(place // NZ, place % NZ, k))
    for step in range(1, 4):
        greet((f, lax.rem(y + step, 4) * 2 + x_hi))
    y_from = lax.rem(z - lax.rem(t, NZ) + 2 + y + 4, 4)
    for core in range(2):
        for side in range(2):
            greet((2 * t + core, y_from * 2 + side))
    grad_loads[1].start()

    def remote(src, dst, send, recv, device):
        return pltpu.make_async_remote_copy(
            src_ref=src, dst_ref=dst, send_sem=send, recv_sem=recv, device_id=device, device_id_type=MESH
        )

    def wait_bytes(ref, sem):
        pltpu.make_async_copy(ref, ref, sem).wait()

    def core_copy(step):
        return remote(
            part.at[step, pl.ds(given, ROWS)],
            from_core.at[step],
            send_sem.at[0],
            core_sem.at[step],
            other_core,
        )

    def own_rows(half, dx, dz, first, count):
        rows = pl.ds(pl.multiple_of(own + first, 16), count)
        return part.at[half * SLABS + SLOT[dx, dz], rows]

    def add_own(half, dx, dz, first, src, begin, count):
        ref = own_rows(half, dx, dz, first, count)
        ref[...] = ref[...] + src[pl.ds(begin, count), :]

    over_x = [
        [
            remote(
                own_rows(half, 1, dz, 0, X_ROWS),
                from_x.at[half, dz],
                send_sem.at[1],
                x_sem.at[half, dz],
                other_x,
            )
            for dz in range(NZ)
        ]
        for half in range(2)
    ]
    last_x = [
        remote(
            own_rows(half, 1, 0, X_ROWS, Z_ROWS),
            from_x_last.at[half],
            send_sem.at[2],
            x_sem.at[half, NZ],
            other_x,
        )
        for half in range(2)
    ]

    class Stream:
        def __init__(self, half, number, near, far):
            dx, first, count, cut = STREAMS[number]
            rest = count - cut
            self.half, self.dx, self.first, self.count, self.cut, self.rest = half, dx, first, count, cut, rest
            self.near, self.far = near.at[half], far.at[half]

            def send(dz, begin, size, dst, n, device):
                return remote(
                    own_rows(half, dx, dz, first + begin, size),
                    dst,
                    send_sem.at[3 + 2 * number + n // 2],
                    z_sem.at[half, number, n],
                    device,
                )

            near, far = self.near, self.far
            self.far_up = send(2, 0, cut, far.at[pl.ds(0, cut)], 0, up)
            self.far_down = send(2, cut, rest, far.at[pl.ds(cut, rest)], 1, down)
            self.up_free = send(1, cut, rest, near.at[0, pl.ds(cut, rest)], 2, up)
            self.up_late = send(1, 0, cut, near.at[0, pl.ds(0, cut)], 2, up)
            self.down_free = send(3, 0, cut, near.at[1, pl.ds(0, cut)], 2, down)
            self.down_late = send(3, cut, rest, near.at[1, pl.ds(cut, rest)], 2, down)
            self.near_sem = z_sem.at[half, number, 2]

        def start_far(self):
            self.far_up.start()
            self.far_down.start()

        def pass_far(self):
            self.far_up.wait_recv()
            add_own(self.half, self.dx, 1, self.first, self.far, 0, self.cut)
            self.up_late.start()
            self.far_down.wait_recv()
            add_own(self.half, self.dx, 3, self.first + self.cut, self.far, self.cut, self.rest)
            self.down_late.start()

        def wait_near(self):
            wait_bytes(self.near, self.near_sem)

    zo = [Stream(half, 0, zo_near, zo_far) for half in range(2)]
    zs = [Stream(half, 1, zs_near, zs_far) for half in range(2)]
    xs = [Stream(half, 2, xs_near, xs_far) for half in range(2)]

    def send_slab(step):
        half, (dx, dz) = step // SLABS, ORDER[step % SLABS]
        if dx == 1:
            over_x[half][dz].start()
        stream = zo[half] if dx == 1 else zs[half]
        if dz == 2:
            stream.start_far()
        if dz == 1:
            stream.up_free.start()
        if dz == 3:
            stream.down_free.start()

    def add_x(half, dz):
        over_x[half][dz].wait_recv()
        add_own(half, 0, dz, 0, from_x.at[half, dz], 0, X_ROWS)

    def x_far(half):
        add_x(half, 2)
        xs[half].start_far()

    def x_up(half):
        add_x(half, 1)
        xs[half].up_free.start()

    def x_down(half):
        add_x(half, 3)
        xs[half].down_free.start()

    def send_last(half):
        zo[half].wait_near()
        ref = own_rows(half, 1, 0, X_ROWS, Z_ROWS)
        ref[...] = ref[...] + zo_near[half, 0] + zo_near[half, 1]
        last_x[half].start()

    def split_heads():
        for copy in late_loads[:6]:
            copy.wait()
        for head in range(8):
            heads[pl.ds(8 * head, 8), :] = query[:, pl.ds(HEAD_SIZE * head, HEAD_SIZE)].astype(jnp.float32)
        fresh[0] = new_key[...].astype(jnp.float32)
        fresh[1] = new_value[...].astype(jnp.float32)

    score_scale = 1.0 / HEAD_SIZE**0.5

    def attend(row):
        own_heads = heads[pl.ds(row, 8, stride=8), :]
        scores = (
            lax.dot_general(
                own_heads.astype(jnp.bfloat16),
                keys[row, 0],
                (((1,), (1,)), ((), ())),
                preferred_element_type=jnp.float32,
            )
            * score_scale
        )
        slots = lax.broadcasted_iota(jnp.int32, (8, CACHE_SLOTS), 1)
        scores = jnp.where(slots < lengths[row], scores, -jnp.inf)
        new_score = (
            jnp.sum(own_heads * fresh[0, pl.ds(row, 1), :], axis=-1, keepdims=True) * score_scale
        )
        top = jnp.maximum(jnp.max(scores, axis=-1, keepdims=True), new_score)
        expo = jnp.exp(scores - top)
        expo_new = jnp.exp(new_score - top)
        total = jnp.sum(expo, axis=-1, keepdims=True) + expo_new
        probs = (expo / total).astype(jnp.bfloat16)
        prob_new = (expo_new / total).astype(jnp.bfloat16).astype(jnp.float32)
        mixed[pl.ds(row, 8, stride=8), :] = (
            jnp.dot(probs, values[row, 0], preferred_element_type=jnp.float32)
            + prob_new * fresh[1, pl.ds(row, 1), :]
        )

    here = chip(0, 0)
    gathers = [
        remote(
            attended.at[k, here],
            attended.at[k, here],
            attend_sem.at[0],
            attend_sem.at[1],
            at(place // NZ, place % NZ, k),
        )
        for place in range(1, NX * NZ)
    ]
    swap = remote(
        attended.at[k], attended.at[k], attend_sem.at[2], attend_sem.at[3], other_core
    )

    def send_attended():
        halves = [
            jnp.concatenate(
                [mixed[pl.ds(8 * head, 8), :] for head in range(4 * half, 4 * half + 4)], axis=1
            )
            for half in range(2)
        ]
        attended[k, here] = jnp.concatenate(halves, axis=0).astype(jnp.bfloat16)
        for copy in gathers:
            copy.start()

    first_row = 3
    after = {
        4: [zo[0].pass_far],
        2: [split_heads],
        5: [lambda: x_far(0)],
        8: [lambda: x_up(0), zs[0].pass_far],
        10: [lambda: send_last(0)],
        11: [lambda: x_down(0), send_attended],
        13: [xs[0].pass_far],
    }

    @pl.loop(0, STEPS + 1)
    def _(step):
        @pl.when(step < SLABS)
        def _():
            pltpu.make_async_copy(
                grad_hbm.at[:, pl.ds(0, 2 * ROWS)], grads.at[step], grad_sem.at[step]
            ).wait()

        for half in range(2):
            @pl.when(step == half * SLABS)
            def _():
                attn_loads[half].wait()

        for slot in range(2, SLABS):
            @pl.when(step == slot - 2)
            def _():
                grad_loads[slot].start()
                if slot == 2:
                    for copy in late_loads[:6]:
                        copy.start()
                if slot == 4:
                    attn_loads[1].start()
                if slot == 6:
                    for copy in late_loads[6:]:
                        copy.start()

        @pl.when(step < STEPS)
        def _():
            part[step] = lax.dot_general(
                grads[lax.rem(step, SLABS)],
                attn[step // SLABS],
                (((0,), (0,)), ((), ())),
                preferred_element_type=jnp.float32,
            ).astype(jnp.bfloat16)

        @pl.when(step == 0)
        def _():
            pl.semaphore_wait(barrier, 1 + 7 + 3 + 4)

        @pl.when(step < STEPS)
        def _():
            core_copy(step).start()

        @pl.when(step > 0)
        def _():
            done = step - 1
            core_copy(done).wait_recv()
            rows = pl.ds(own, ROWS)
            part[done, rows, :] = part[done, rows, :] + from_core[done]

        for done in range(STEPS):
            @pl.when(step == done + 1)
            def _():
                send_slab(done)
                for action in after.get(done, ()):
                    action()

        @pl.when(jnp.logical_and(step > first_row, step <= first_row + 8))
        def _():
            attend(step - first_row - 1)

    x_far(1)
    zo[1].pass_far()
    x_up(1)
    zs[1].pass_far()
    x_down(1)
    weights[:, pl.ds(ROWS, PADDED - ROWS), :] = jnp.zeros((2, PADDED - ROWS, HALF), jnp.bfloat16)
    for copy in late_loads[6:]:
        copy.wait()

    def adam(half, first, count, terms):
        columns = pl.ds(HALF * half, HALF)

        @pl.loop(0, count // 16)
        def _(n):
            begin = pl.multiple_of(n * 16, 16)
            rows = pl.ds(pl.multiple_of(first + begin, 16), 16)
            mine = pl.ds(pl.multiple_of(own + first + begin, 16), 16)
            total = part[half * SLABS + SLOT[0, 0], mine, :].astype(jnp.float32)
            for term in terms:
                total = total + term[pl.ds(begin, 16), :].astype(jnp.float32)
            grad = total * (1.0 / TOKENS)
            one_new = beta_one * one[rows, columns] + (1.0 - beta_one) * grad
            two_new = beta_two * two[rows, columns] + (1.0 - beta_two) * grad * grad
            update = (one_new * (1.0 / bias_one)) / (jnp.sqrt(two_new * (1.0 / bias_two)) + adam_eps)
            master_new = master[rows, columns] * (1.0 - learn_rate * weight_decay) - learn_rate * update
            one_out[rows, columns] = one_new
            two_out[rows, columns] = two_new
            master_out[rows, columns] = master_new
            weights[half, rows, :] = master_new.astype(jnp.bfloat16)

    def adam_x(half):
        xs[half].wait_near()
        over_x[half][0].wait_recv()
        adam(half, 0, X_ROWS, (from_x.at[half, 0], xs_near.at[half, 0], xs_near.at[half, 1]))

    def adam_z(half):
        zs[half].wait_near()
        last_x[half].wait_recv()
        adam(half, X_ROWS, Z_ROWS, (from_x_last.at[half], zs_near.at[half, 0], zs_near.at[half, 1]))

    def product(half):
        return lax.dot_general(
            attended[...].reshape(256, HALF),
            weights[half],
            (((1,), (1,)), ((), ())),
            preferred_element_type=jnp.float32,
        ).reshape(2, 8, 16, PADDED)[:, :, 8 * half : 8 * half + 8, :]

    adam_x(0)
    send_last(1)
    xs[1].pass_far()
    wait_bytes(attended.at[k, pl.ds(0, 7)], attend_sem.at[1])
    swap.start()
    adam_z(0)
    swap.wait_recv()
    share = product(0)
    adam_x(1)
    adam_z(1)
    share = share + product(1)

    for place in range(NZ):
        shares[place] = jnp.concatenate(
            [share[core, dx * NZ + place] for dx in range(NX) for core in range(2)], axis=0
        ).astype(jnp.bfloat16)
    for step in range(1, 4):
        remote(
            shares.at[lax.rem(z_summed + step, NZ)],
            arrived.at[step - 1],
            share_sem.at[0],
            share_sem.at[1],
            (f, lax.rem(y + step, 4) * 2 + x_hi),
        ).start()
    wait_bytes(arrived, share_sem.at[1])
    total = shares[z_summed].astype(jnp.float32)
    for step in range(3):
        total = total + arrived[step].astype(jnp.float32)
    totals[...] = total
    for dx in range(NX):
        for core in range(2):
            remote(
                totals.at[pl.ds(8 * (2 * dx + core), 8)],
                decoded.at[k, x_hi],
                share_sem.at[2],
                share_sem.at[3],
                ((dx * NZ + z_summed) * 2 + core, f // 2),
            ).start()

    wait_bytes(from_core, send_sem.at[0])
    wait_bytes(from_x, send_sem.at[1])
    wait_bytes(from_x_last, send_sem.at[2])
    for number, (near, far) in enumerate(((zo_near, zo_far), (zs_near, zs_far), (xs_near, xs_far))):
        wait_bytes(far, send_sem.at[3 + 2 * number])
        wait_bytes(near, send_sem.at[4 + 2 * number])
    wait_bytes(attended.at[k, pl.ds(0, 7)], attend_sem.at[0])
    swap.wait_send()
    wait_bytes(arrived, share_sem.at[0])
    wait_bytes(decoded, share_sem.at[2])
    wait_bytes(decoded, share_sem.at[3])
    decoded_out[...] = decoded[:, 0] + decoded[:, 1]


def write_kernel(master, one, two, decoded, master_out, one_out, two_out, decoded_out, rounded, sems):
    stores = [
        pltpu.make_async_copy(src, dst, sems.at[n])
        for n, (src, dst) in enumerate(((master, master_out), (one, one_out), (two, two_out)))
    ]
    for copy in stores:
        copy.start()
    rounded[...] = jnp.concatenate(
        [decoded[core, :, :ROWS] for core in range(2)], axis=1
    ).astype(jnp.bfloat16)
    stores.append(pltpu.make_async_copy(rounded, decoded_out, sems.at[3]))
    stores[3].start()
    for copy in stores:
        copy.wait()


def shards(*args):
    bf16, f32 = jnp.bfloat16, jnp.float32
    vmem = pl.BlockSpec(memory_space=pltpu.VMEM)
    anywhere = pl.BlockSpec(memory_space=pl.ANY)
    results = pl.pallas_call(
        kernel,
        out_shape=(
            pltpu.VMEM((ROWS, COLS), f32),
            pltpu.VMEM((ROWS, COLS), f32),
            pltpu.VMEM((ROWS, COLS), f32),
            pltpu.VMEM((2, 8, PADDED), f32),
        ),
        in_specs=[anywhere] * 11,
        out_specs=(vmem,) * 4,
        scratch_shapes=[
            pltpu.VMEM((2, 1024, HALF), bf16),
            pltpu.VMEM((SLABS, 1024, 2 * ROWS), bf16),
            pltpu.VMEM((STEPS, 2 * ROWS, HALF), bf16),
            pltpu.VMEM((STEPS, ROWS, HALF), bf16),
            pltpu.VMEM((2, NZ, X_ROWS, HALF), bf16),
            pltpu.VMEM((2, Z_ROWS, HALF), bf16),
            pltpu.VMEM((2, 2, Z_ROWS, HALF), bf16),
            pltpu.VMEM((2, Z_ROWS, HALF), bf16),
            pltpu.VMEM((2, 2, Z_ROWS, HALF), bf16),
            pltpu.VMEM((2, Z_ROWS, HALF), bf16),
            pltpu.VMEM((2, 2, X_ROWS, HALF), bf16),
            pltpu.VMEM((2, X_ROWS, HALF), bf16),
            pltpu.VMEM((ROWS, COLS), f32),
            pltpu.VMEM((ROWS, COLS), f32),
            pltpu.VMEM((ROWS, COLS), f32),
            pltpu.VMEM((8, 1024), bf16),
            pltpu.VMEM((8, HEAD_SIZE), bf16),
            pltpu.VMEM((8, HEAD_SIZE), bf16),
            pltpu.VMEM((8, 1, CACHE_SLOTS, HEAD_SIZE), bf16),
            pltpu.VMEM((8, 1, CACHE_SLOTS, HEAD_SIZE), bf16),
            pltpu.SMEM((8,), jnp.int32),
            pltpu.VMEM((2, PADDED, HALF), bf16),
            pltpu.VMEM((64, HEAD_SIZE), f32),
            pltpu.VMEM((64, HEAD_SIZE), f32),
            pltpu.VMEM((2, 8, HEAD_SIZE), f32),
            pltpu.VMEM((2, 8, 16, HALF), bf16),
            pltpu.VMEM((NZ, 32, PADDED), bf16),
            pltpu.VMEM((3, 32, PADDED), bf16),
            pltpu.VMEM((32, PADDED), f32),
            pltpu.VMEM((2, 2, 8, PADDED), f32),
            pltpu.SemaphoreType.DMA((9,)),
            pltpu.SemaphoreType.DMA((2,)),
            pltpu.SemaphoreType.DMA((SLABS,)),
            pltpu.SemaphoreType.DMA((STEPS,)),
            pltpu.SemaphoreType.DMA((2, NZ + 1)),
            pltpu.SemaphoreType.DMA((2, 3, 3)),
            pltpu.SemaphoreType.DMA((4,)),
            pltpu.SemaphoreType.DMA((4,)),
            pltpu.SemaphoreType.DMA((9,)),
        ],
        compiler_params=pltpu.CompilerParams(
            collective_id=0, has_side_effects=True, vmem_limit_bytes=50 << 20
        ),
        cost_estimate=pl.CostEstimate(
            flops=2 * 1024 * 1024 * 5120, bytes_accessed=24 << 20, transcendentals=1 << 19
        ),
    )(*(pltpu.with_memory_space_constraint(arg, pltpu.HBM) for arg in args))
    return pl.pallas_call(
        write_kernel,
        out_shape=(
            jax.ShapeDtypeStruct((ROWS, COLS), f32),
            jax.ShapeDtypeStruct((ROWS, COLS), f32),
            jax.ShapeDtypeStruct((ROWS, COLS), f32),
            jax.ShapeDtypeStruct((8, 2 * ROWS), bf16),
        ),
        in_specs=[vmem] * 4,
        out_specs=(anywhere,) * 4,
        scratch_shapes=[pltpu.VMEM((8, 2 * ROWS), bf16), pltpu.SemaphoreType.DMA((4,))],
        compiler_params=pltpu.CompilerParams(vmem_limit_bytes=8 << 20),
        cost_estimate=pl.CostEstimate(flops=0, bytes_accessed=8 << 20, transcendentals=0),
    )(*results)


def solution(mesh):
    placed = (
        P("fsdp", "tp"),
        P("fsdp", None),
        P("fsdp", "tp"),
        P("fsdp", "tp"),
        P("fsdp", "tp"),
        P("fsdp", "tp"),
        P("fsdp", "tp"),
        P("fsdp", "tp"),
        P("fsdp", "tp", None, None),
        P("fsdp", "tp", None, None),
        P("fsdp"),
    )
    return jax.shard_map(
        shards,
        mesh=mesh,
        in_specs=placed,
        out_specs=(P("fsdp", "tp"), P("fsdp", "tp"), P("fsdp", "tp"), P("fsdp", "tp")),
        check_vma=False,
    )
```

```python
import jax
import jax.numpy as jnp
from jax import lax
from jax.experimental import pallas as pl
from jax.experimental.pallas import tpu as pltpu
from jax.sharding import PartitionSpec as P

MESH = pl.DeviceIdType.MESH
HEAD_SIZE = 128
CACHE_SLOTS = 1024
TOKENS = 16384

beta_one = 0.9
beta_two = 0.95
learn_rate = 0.003
weight_decay = 0.1
adam_eps = 1e-08
bias_one = 1.0 - 0.9**10
bias_two = 1.0 - 0.95**10

NX, NZ = 2, 4
ROWS = 320
COLS = 1024
HALF = COLS // 2
EARLY = 256
PADDED = 384
ORDER = ((1, 2), (1, 1), (1, 3), (0, 2), (0, 1), (0, 3), (1, 0), (0, 0))
SLABS = len(ORDER)
SLOT = {place: slot for slot, place in enumerate(ORDER)}
STREAMS = (
    ((1, 112, 144, 80), (0, 112, 144, 80), (0, 0, 112, 48)),
    ((1, 288, 32, 16), (0, 288, 32, 16), (0, 256, 32, 16)),
)
Z_TOTAL = sum(chunk[0][2] for chunk in STREAMS)
X_TOTAL = sum(chunk[2][2] for chunk in STREAMS)
Z_BEGIN = (0, STREAMS[0][0][2])
X_BEGIN = (0, STREAMS[0][2][2])


def kernel(
    attn_hbm,
    grad_hbm,
    master_hbm,
    one_hbm,
    two_hbm,
    query_hbm,
    new_key_hbm,
    new_value_hbm,
    keys_hbm,
    values_hbm,
    lengths_hbm,
    master_out,
    one_out,
    two_out,
    decoded_out,
    attn,
    grads,
    part,
    from_core,
    from_x,
    from_x_last,
    zo_near,
    zo_far,
    zs_near,
    zs_far,
    xs_near,
    xs_far,
    state,
    query,
    new_key,
    new_value,
    caches,
    lengths,
    weights,
    heads,
    mixed,
    fresh,
    attended,
    shares,
    arrived,
    totals,
    decoded,
    late_shares,
    late_arrived,
    load_sem,
    attn_sem,
    grad_sem,
    core_sem,
    x_sem,
    z_sem,
    attend_sem,
    share_sem,
    late_sem,
    send_sem,
):
    f = lax.axis_index("fsdp")
    t = lax.axis_index("tp")
    x, z, k = f // (2 * NZ), lax.rem(f // 2, NZ), lax.rem(f, 2)
    y, x_hi = t // 2, lax.rem(t, 2)
    z_summed = lax.rem(z + 2 + y - f // 4 + 8, NZ)

    def chip(dx, dz):
        return lax.rem(x + dx, NX) * NZ + lax.rem(z + dz, NZ)

    def at(dx, dz, core):
        return (chip(dx, dz) * 2 + core, t)

    other_core = at(0, 0, 1 - k)
    other_x = at(1, 0, k)
    up, down = at(0, 1, k), at(0, 3, k)
    own = pl.multiple_of(k * ROWS, 64)
    given = pl.multiple_of((1 - k) * ROWS, 64)

    attn_loads = [
        pltpu.make_async_copy(
            attn_hbm.at[:, pl.ds(HALF * half, HALF)], attn.at[:, pl.ds(HALF * half, HALF)], attn_sem.at[half]
        )
        for half in range(2)
    ]
    grad_loads = []
    for slot, (dx, dz) in enumerate(ORDER):
        columns = pl.ds(pl.multiple_of(chip(dx, dz) * 2 * ROWS, 128), 2 * ROWS)
        grad_loads.append(
            pltpu.make_async_copy(grad_hbm.at[:, columns], grads.at[slot], grad_sem.at[slot])
        )
    late_loads = [
        pltpu.make_async_copy(src, dst, load_sem.at[n])
        for n, (src, dst) in enumerate(
            (
                (query_hbm, query),
                (new_key_hbm, new_key),
                (new_value_hbm, new_value),
                (lengths_hbm, lengths),
            )
        )
    ]
    late_loads += [
        pltpu.make_async_copy(keys_hbm, caches.at[0], load_sem.at[4]),
        pltpu.make_async_copy(values_hbm, caches.at[1], load_sem.at[4]),
        pltpu.make_async_copy(master_hbm, state.at[0], load_sem.at[5]),
        pltpu.make_async_copy(one_hbm, state.at[1], load_sem.at[5]),
        pltpu.make_async_copy(two_hbm, state.at[2], load_sem.at[5]),
    ]
    first_columns = pl.ds(pl.multiple_of(chip(*ORDER[0]) * 2 * ROWS, 128), 2 * ROWS)
    for piece in range(4):
        rows = pl.ds(256 * piece, 256)
        pltpu.make_async_copy(
            grad_hbm.at[rows, first_columns], grads.at[0, rows], grad_sem.at[0]
        ).start()
        pltpu.make_async_copy(
            attn_hbm.at[rows, pl.ds(0, HALF)], attn.at[rows, pl.ds(0, HALF)], attn_sem.at[0]
        ).start()

    barrier = pltpu.get_barrier_semaphore()

    def greet(device):
        pl.semaphore_signal(barrier, inc=1, device_id=device, device_id_type=MESH)

    greet(other_core)
    for place in range(1, NX * NZ):
        greet(at(place // NZ, place % NZ, k))
    for step in range(1, 4):
        greet((f, lax.rem(y + step, 4) * 2 + x_hi))
    stays = t == f // 2
    for core in range(2):
        for step in range(8):
            source = (2 * t + core, lax.rem(t + step, 8))
            if step == 0:
                @pl.when(jnp.logical_not(jnp.logical_and(stays, k == core)))
                def _():
                    greet(source)
            else:
                greet(source)
    attn_loads[1].start()

    def remote(src, dst, send, recv, device):
        return pltpu.make_async_remote_copy(
            src_ref=src, dst_ref=dst, send_sem=send, recv_sem=recv, device_id=device, device_id_type=MESH
        )

    def wait_bytes(ref, sem):
        pltpu.make_async_copy(ref, ref, sem).wait()

    def core_copy(slot):
        return remote(
            part.at[slot, pl.ds(given, ROWS)],
            from_core.at[slot],
            send_sem.at[0],
            core_sem.at[slot],
            other_core,
        )

    def own_rows(dx, dz, first, count):
        rows = pl.ds(pl.multiple_of(own + first, 16), count)
        return part.at[SLOT[dx, dz], rows]

    def add_own(dx, dz, first, count, *terms):
        ref = own_rows(dx, dz, first, count)
        for begin in range(0, count, 16):
            rows = pl.ds(begin, 16)
            total = ref[rows, :]
            for term in terms:
                total = total + term[rows, :]
            ref[rows, :] = total

    def x_landing(chunk, dz):
        return from_x.at[dz, pl.ds(X_BEGIN[chunk], STREAMS[chunk][2][2])]

    def x_copy(chunk, dz):
        _, first, count, _ = STREAMS[chunk][2]
        return remote(
            own_rows(1, dz, first, count),
            x_landing(chunk, dz),
            send_sem.at[1],
            x_sem.at[chunk, dz],
            other_x,
        )

    over_x = [[x_copy(chunk, dz) for dz in range(NZ)] for chunk in range(2)]

    def z_landing(chunk):
        return from_x_last.at[pl.ds(Z_BEGIN[chunk], STREAMS[chunk][0][2])]

    def last_copy(chunk):
        _, first, count, _ = STREAMS[chunk][0]
        return remote(
            own_rows(1, 0, first, count),
            z_landing(chunk),
            send_sem.at[2],
            x_sem.at[chunk, NZ],
            other_x,
        )

    last_x = [last_copy(chunk) for chunk in range(2)]

    class Stream:
        def __init__(self, chunk, number, near, far):
            dx, first, count, cut = STREAMS[chunk][number]
            rest = count - cut
            place = pl.ds((X_BEGIN if number == 2 else Z_BEGIN)[chunk], count)
            self.dx, self.first, self.count, self.cut, self.rest = dx, first, count, cut, rest
            self.near, self.far = near.at[:, place], far.at[place]

            def send(dz, begin, size, dst, n, device):
                return remote(
                    own_rows(dx, dz, first + begin, size),
                    dst,
                    send_sem.at[3 + 2 * number + n // 2],
                    z_sem.at[chunk, number, n],
                    device,
                )

            near, far = self.near, self.far
            self.far_up = send(2, 0, cut, far.at[pl.ds(0, cut)], 0, up)
            self.far_down = send(2, cut, rest, far.at[pl.ds(cut, rest)], 1, down)
            self.up_free = send(1, cut, rest, near.at[0, pl.ds(cut, rest)], 2, up)
            self.up_late = send(1, 0, cut, near.at[0, pl.ds(0, cut)], 2, up)
            self.down_free = send(3, 0, cut, near.at[1, pl.ds(0, cut)], 2, down)
            self.down_late = send(3, cut, rest, near.at[1, pl.ds(cut, rest)], 2, down)
            self.near_sem = z_sem.at[chunk, number, 2]

        def start_far(self):
            self.far_up.start()
            self.far_down.start()

        def start_free(self):
            self.up_free.start()
            self.down_free.start()

        def pass_far(self):
            self.far_up.wait_recv()
            add_own(self.dx, 1, self.first, self.cut, self.far.at[pl.ds(0, self.cut)])
            self.up_late.start()
            self.far_down.wait_recv()
            add_own(self.dx, 3, self.first + self.cut, self.rest, self.far.at[pl.ds(self.cut, self.rest)])
            self.down_late.start()

        def wait_near(self):
            wait_bytes(self.near, self.near_sem)

    zo = [Stream(chunk, 0, zo_near, zo_far) for chunk in range(2)]
    zs = [Stream(chunk, 1, zs_near, zs_far) for chunk in range(2)]
    xs = [Stream(chunk, 2, xs_near, xs_far) for chunk in range(2)]

    def add_x(chunk, dz):
        over_x[chunk][dz].wait_recv()
        _, first, count, _ = STREAMS[chunk][2]
        add_own(0, dz, first, count, x_landing(chunk, dz))

    def x_far(chunk):
        add_x(chunk, 2)
        xs[chunk].start_far()

    def x_up(chunk):
        add_x(chunk, 1)
        xs[chunk].up_free.start()

    def x_down(chunk):
        add_x(chunk, 3)
        xs[chunk].down_free.start()

    def send_last(chunk):
        stream = zo[chunk]
        stream.wait_near()
        add_own(1, 0, stream.first, stream.count, stream.near.at[0], stream.near.at[1])
        last_x[chunk].start()

    def split_heads():
        for copy in late_loads[:4]:
            copy.wait()
        wait_bytes(caches, load_sem.at[4])
        for head in range(8):
            heads[pl.ds(8 * head, 8), :] = query[:, pl.ds(HEAD_SIZE * head, HEAD_SIZE)].astype(jnp.float32)
        fresh[0] = new_key[...].astype(jnp.float32)
        fresh[1] = new_value[...].astype(jnp.float32)

    score_scale = 1.0 / HEAD_SIZE**0.5

    def attend(row):
        own_heads = heads[pl.ds(row, 8, stride=8), :]
        scores = (
            lax.dot_general(
                own_heads.astype(jnp.bfloat16),
                caches[0, row, 0],
                (((1,), (1,)), ((), ())),
                preferred_element_type=jnp.float32,
            )
            * score_scale
        )
        slots = lax.broadcasted_iota(jnp.int32, (8, CACHE_SLOTS), 1)
        scores = jnp.where(slots < lengths[row], scores, -jnp.inf)
        new_score = (
            jnp.sum(own_heads * fresh[0, pl.ds(row, 1), :], axis=-1, keepdims=True) * score_scale
        )
        top = jnp.maximum(jnp.max(scores, axis=-1, keepdims=True), new_score)
        expo = jnp.exp(scores - top)
        expo_new = jnp.exp(new_score - top)
        total = jnp.sum(expo, axis=-1, keepdims=True) + expo_new
        probs = (expo / total).astype(jnp.bfloat16)
        prob_new = (expo_new / total).astype(jnp.bfloat16).astype(jnp.float32)
        mixed[pl.ds(row, 8, stride=8), :] = (
            jnp.dot(probs, caches[1, row, 0], preferred_element_type=jnp.float32)
            + prob_new * fresh[1, pl.ds(row, 1), :]
        )

    here = chip(0, 0)
    gathers = [
        remote(
            attended.at[k, here],
            attended.at[k, here],
            attend_sem.at[0],
            attend_sem.at[1],
            at(place // NZ, place % NZ, k),
        )
        for place in range(1, NX * NZ)
    ]
    swap = remote(
        attended.at[k], attended.at[k], attend_sem.at[2], attend_sem.at[3], other_core
    )

    def send_attended():
        halves = [
            jnp.concatenate(
                [mixed[pl.ds(8 * head, 8), :] for head in range(4 * half, 4 * half + 4)], axis=1
            )
            for half in range(2)
        ]
        attended[k, here] = jnp.concatenate(halves, axis=0).astype(jnp.bfloat16)
        for copy in gathers:
            copy.start()

    after = (
        None,
        (over_x[0][1].start, zo[0].up_free.start, over_x[1][1].start, zo[1].up_free.start, split_heads),
        (over_x[0][3].start, zo[0].down_free.start, zo[1].down_free.start, zo[0].pass_far),
        (zs[0].start_far, zo[1].pass_far, lambda: x_far(0)),
        (zs[0].up_free.start,),
        (zs[0].down_free.start, lambda: x_up(0)),
        (send_attended, over_x[0][0].start, lambda: send_last(0)),
        (),
    )
    first_row = 3

    def first_core_copy(half):
        columns = pl.ds(HALF * half, HALF)
        return remote(
            part.at[0, pl.ds(given, ROWS), columns],
            from_core.at[0, :, columns],
            send_sem.at[0],
            core_sem.at[SLABS * half],
            other_core,
        )

    def slab_half(slot, half, rows):
        columns = pl.ds(HALF * half, HALF)
        part[slot, rows, columns] = lax.dot_general(
            grads[slot, :, rows], attn[:, columns], (((0,), (0,)), ((), ())), preferred_element_type=jnp.float32
        ).astype(jnp.bfloat16)

    def send_first(half):
        columns = pl.ds(HALF * half, HALF)
        first_core_copy(half).wait_recv()
        for begin in range(0, ROWS, 16):
            rows = pl.ds(pl.multiple_of(own + begin, 16), 16)
            part[0, rows, columns] = part[0, rows, columns] + from_core[0, pl.ds(begin, 16), columns]
        _, first, count, _ = STREAMS[0][2]
        remote(
            own_rows(1, 2, first, count).at[:, columns],
            x_landing(0, 2).at[:, columns],
            send_sem.at[1],
            x_sem.at[0, 2],
            other_x,
        ).start()
        _, first, count, cut = STREAMS[0][0]
        for n, begin, size, device in ((0, 0, cut, up), (1, cut, count - cut, down)):
            remote(
                own_rows(1, 2, first + begin, size).at[:, columns],
                zo[0].far.at[pl.ds(begin, size), columns],
                send_sem.at[3],
                z_sem.at[0, 0, n],
                device,
            ).start()

    grad_loads[0].wait()
    for half in range(2):
        attn_loads[half].wait()
        slab_half(0, half, pl.ds(pl.multiple_of((1 - k) * 256, 128), 384))
        if half == 0:
            pl.semaphore_wait(barrier, 1 + 7 + 3 + 16 - stays.astype(jnp.int32))
            grad_loads[1].start()
        first_core_copy(half).start()
        slab_half(0, half, pl.ds(pl.multiple_of(k * 384, 128), 256))
    grad_loads[2].start()
    for copy in late_loads[:6]:
        copy.start()
    send_first(0)
    grad_loads[1].wait()
    slab_half(1, 0, pl.ds(0, 2 * ROWS))
    send_first(1)
    over_x[1][2].start()
    zo[1].start_far()
    slab_half(1, 1, pl.ds(0, 2 * ROWS))
    core_copy(1).start()
    grad_loads[3].start()

    @pl.loop(2, SLABS + 1)
    def _(step):
        @pl.when(step < SLABS)
        def _():
            pltpu.make_async_copy(
                grad_hbm.at[:, pl.ds(0, 2 * ROWS)], grads.at[step], grad_sem.at[step]
            ).wait()

        for slot in range(4, SLABS):
            @pl.when(step == slot - 2)
            def _():
                grad_loads[slot].start()
                if slot == 6:
                    for copy in late_loads[6:]:
                        copy.start()

        @pl.when(step < SLABS)
        def _():
            part[step] = lax.dot_general(
                grads[step], attn[...], (((0,), (0,)), ((), ())), preferred_element_type=jnp.float32
            ).astype(jnp.bfloat16)
            core_copy(step).start()

        done = step - 1
        core_copy(done).wait_recv()
        rows = pl.ds(own, ROWS)
        part[done, rows, :] = part[done, rows, :] + from_core[done]

        for slot in range(1, SLABS):
            @pl.when(step == slot + 1)
            def _():
                for action in after[slot]:
                    action()

        @pl.when(jnp.logical_and(step >= first_row, step < first_row + 4))
        def _():
            attend(2 * (step - first_row))
            attend(2 * (step - first_row) + 1)

    zs[0].pass_far()
    x_down(0)
    xs[0].pass_far()
    zs[1].start_far()
    x_far(1)
    zs[1].start_free()
    x_up(1)
    over_x[1][3].start()
    over_x[1][0].start()
    send_last(1)
    wait_bytes(attended.at[k, pl.ds(0, 7)], attend_sem.at[1])
    swap.start()
    weights[pl.ds(ROWS, PADDED - ROWS), :] = jnp.zeros((PADDED - ROWS, COLS), jnp.bfloat16)
    wait_bytes(state, load_sem.at[5])

    def adam(first, count, terms):
        @pl.loop(0, count // 16)
        def _(n):
            begin = pl.multiple_of(n * 16, 16)
            rows = pl.ds(pl.multiple_of(first + begin, 16), 16)
            mine = pl.ds(pl.multiple_of(own + first + begin, 16), 16)
            total = part[SLOT[0, 0], mine, :].astype(jnp.float32)
            for term in terms:
                total = total + term[pl.ds(begin, 16), :].astype(jnp.float32)
            grad = total * (1.0 / TOKENS)
            one_new = beta_one * state[1, rows, :] + (1.0 - beta_one) * grad
            two_new = beta_two * state[2, rows, :] + (1.0 - beta_two) * grad * grad
            update = (one_new * (1.0 / bias_one)) / (jnp.sqrt(two_new * (1.0 / bias_two)) + adam_eps)
            master_new = state[0, rows, :] * (1.0 - learn_rate * weight_decay) - learn_rate * update
            one_out[rows, :] = one_new
            two_out[rows, :] = two_new
            master_out[rows, :] = master_new
            weights[rows, :] = master_new.astype(jnp.bfloat16)

    def adam_x(chunk):
        xs[chunk].wait_near()
        over_x[chunk][0].wait_recv()
        _, first, count, _ = STREAMS[chunk][2]
        adam(first, count, (x_landing(chunk, 0), xs[chunk].near.at[0], xs[chunk].near.at[1]))

    def adam_z(chunk):
        zs[chunk].wait_near()
        last_x[chunk].wait_recv()
        _, first, count, _ = STREAMS[chunk][1]
        adam(first, count, (z_landing(chunk), zs[chunk].near.at[0], zs[chunk].near.at[1]))

    def product(first, count):
        halves = [
            lax.dot_general(
                attended[...].reshape(256, HALF),
                weights[pl.ds(first, count), pl.ds(HALF * half, HALF)],
                (((1,), (1,)), ((), ())),
                preferred_element_type=jnp.float32,
            ).reshape(2, 8, 16, count)[:, :, 8 * half : 8 * half + 8, :]
            for half in range(2)
        ]
        return halves[0] + halves[1]

    adam_z(0)
    adam_x(0)
    swap.wait_recv()
    share = product(0, EARLY)
    for place in range(NZ):
        shares[place] = jnp.concatenate(
            [share[core, dx * NZ + place] for dx in range(NX) for core in range(2)], axis=0
        ).astype(jnp.bfloat16)

    for step in (2, 1, 3):
        remote(
            shares.at[lax.rem(z_summed + step, NZ)],
            arrived.at[step - 1],
            share_sem.at[0],
            share_sem.at[1],
            (f, lax.rem(y + step, 4) * 2 + x_hi),
        ).start()

    zs[1].pass_far()
    x_down(1)
    xs[1].pass_far()
    adam_z(1)
    adam_x(1)
    late_shares[...] = product(EARLY, PADDED - EARLY).reshape(16, 8, PADDED - EARLY)

    def late_copy(step):
        target = lax.rem(f + step, 16)
        return remote(
            late_shares.at[lax.rem(target, 2) * 8 + target // 2],
            late_arrived.at[k, t],
            late_sem.at[0],
            late_sem.at[1],
            (target, f // 2),
        )

    for step in range(1, 16):
        late_copy(step).start()

    @pl.when(stays)
    def _():
        pltpu.make_async_copy(
            late_shares.at[k * 8 + f // 2], late_arrived.at[k, t], late_sem.at[1]
        ).start()

    @pl.when(jnp.logical_not(stays))
    def _():
        late_copy(0).start()

    wait_bytes(arrived, share_sem.at[1])
    total = shares[z_summed].astype(jnp.float32)
    for step in range(3):
        total = total + arrived[step].astype(jnp.float32)
    totals[...] = total
    for dx in range(NX):
        for core in range(2):
            remote(
                totals.at[pl.ds(8 * (2 * dx + core), 8)],
                decoded.at[k, x_hi],
                share_sem.at[2],
                share_sem.at[3],
                ((dx * NZ + z_summed) * 2 + core, f // 2),
            ).start()

    wait_bytes(from_core, send_sem.at[0])
    wait_bytes(from_x, send_sem.at[1])
    wait_bytes(from_x_last, send_sem.at[2])
    for number, (near, far) in enumerate(((zo_near, zo_far), (zs_near, zs_far), (xs_near, xs_far))):
        wait_bytes(far, send_sem.at[3 + 2 * number])
        wait_bytes(near, send_sem.at[4 + 2 * number])
    wait_bytes(attended.at[k, pl.ds(0, 7)], attend_sem.at[0])
    swap.wait_send()
    wait_bytes(arrived, share_sem.at[0])
    wait_bytes(decoded, share_sem.at[2])

    @pl.when(stays)
    def _():
        wait_bytes(late_shares.at[pl.ds(0, 15)], late_sem.at[0])

    @pl.when(jnp.logical_not(stays))
    def _():
        wait_bytes(late_shares, late_sem.at[0])

    wait_bytes(decoded, share_sem.at[3])
    decoded_out[:, :, pl.ds(0, EARLY)] = decoded[:, 0] + decoded[:, 1]
    wait_bytes(late_arrived, late_sem.at[1])
    decoded_out[:, :, pl.ds(EARLY, PADDED - EARLY)] = jnp.sum(late_arrived[...], axis=1)


def write_kernel(master, one, two, decoded, master_out, one_out, two_out, decoded_out, rounded, sems):
    pairs = ((master, master_out), (one, one_out), (two, two_out))
    for piece in range(4):
        rows = pl.ds(ROWS // 4 * piece, ROWS // 4)
        for n, (src, dst) in enumerate(pairs):
            pltpu.make_async_copy(src.at[rows], dst.at[rows], sems.at[n]).start()
    rounded[...] = jnp.concatenate(
        [decoded[core, :, :ROWS] for core in range(2)], axis=1
    ).astype(jnp.bfloat16)
    last = pltpu.make_async_copy(rounded, decoded_out, sems.at[3])
    last.start()
    for n, (src, dst) in enumerate(pairs):
        pltpu.make_async_copy(src, dst, sems.at[n]).wait()
    last.wait()


def shards(*args):
    bf16, f32 = jnp.bfloat16, jnp.float32
    vmem = pl.BlockSpec(memory_space=pltpu.VMEM)
    anywhere = pl.BlockSpec(memory_space=pl.ANY)
    results = pl.pallas_call(
        kernel,
        out_shape=(
            pltpu.VMEM((ROWS, COLS), f32),
            pltpu.VMEM((ROWS, COLS), f32),
            pltpu.VMEM((ROWS, COLS), f32),
            pltpu.VMEM((2, 8, PADDED), f32),
        ),
        in_specs=[anywhere] * 11,
        out_specs=(vmem,) * 4,
        scratch_shapes=[
            pltpu.VMEM((1024, COLS), bf16),
            pltpu.VMEM((SLABS, 1024, 2 * ROWS), bf16),
            pltpu.VMEM((SLABS, 2 * ROWS, COLS), bf16),
            pltpu.VMEM((SLABS, ROWS, COLS), bf16),
            pltpu.VMEM((NZ, X_TOTAL, COLS), bf16),
            pltpu.VMEM((Z_TOTAL, COLS), bf16),
            pltpu.VMEM((2, Z_TOTAL, COLS), bf16),
            pltpu.VMEM((Z_TOTAL, COLS), bf16),
            pltpu.VMEM((2, Z_TOTAL, COLS), bf16),
            pltpu.VMEM((Z_TOTAL, COLS), bf16),
            pltpu.VMEM((2, X_TOTAL, COLS), bf16),
            pltpu.VMEM((X_TOTAL, COLS), bf16),
            pltpu.VMEM((3, ROWS, COLS), f32),
            pltpu.VMEM((8, 1024), bf16),
            pltpu.VMEM((8, HEAD_SIZE), bf16),
            pltpu.VMEM((8, HEAD_SIZE), bf16),
            pltpu.VMEM((2, 8, 1, CACHE_SLOTS, HEAD_SIZE), bf16),
            pltpu.SMEM((8,), jnp.int32),
            pltpu.VMEM((PADDED, COLS), bf16),
            pltpu.VMEM((64, HEAD_SIZE), f32),
            pltpu.VMEM((64, HEAD_SIZE), f32),
            pltpu.VMEM((2, 8, HEAD_SIZE), f32),
            pltpu.VMEM((2, 8, 16, HALF), bf16),
            pltpu.VMEM((NZ, 32, EARLY), bf16),
            pltpu.VMEM((3, 32, EARLY), bf16),
            pltpu.VMEM((32, EARLY), f32),
            pltpu.VMEM((2, 2, 8, EARLY), f32),
            pltpu.VMEM((16, 8, PADDED - EARLY), f32),
            pltpu.VMEM((2, 8, 8, PADDED - EARLY), f32),
            pltpu.SemaphoreType.DMA((6,)),
            pltpu.SemaphoreType.DMA((2,)),
            pltpu.SemaphoreType.DMA((SLABS,)),
            pltpu.SemaphoreType.DMA((SLABS + 1,)),
            pltpu.SemaphoreType.DMA((2, NZ + 1)),
            pltpu.SemaphoreType.DMA((2, 3, 3)),
            pltpu.SemaphoreType.DMA((4,)),
            pltpu.SemaphoreType.DMA((4,)),
            pltpu.SemaphoreType.DMA((2,)),
            pltpu.SemaphoreType.DMA((9,)),
        ],
        compiler_params=pltpu.CompilerParams(
            collective_id=0, has_side_effects=True, vmem_limit_bytes=50 << 20
        ),
        cost_estimate=pl.CostEstimate(
            flops=2 * 1024 * 1024 * 5120, bytes_accessed=24 << 20, transcendentals=1 << 19
        ),
    )(*(pltpu.with_memory_space_constraint(arg, pltpu.HBM) for arg in args))
    return pl.pallas_call(
        write_kernel,
        out_shape=(
            jax.ShapeDtypeStruct((ROWS, COLS), f32),
            jax.ShapeDtypeStruct((ROWS, COLS), f32),
            jax.ShapeDtypeStruct((ROWS, COLS), f32),
            jax.ShapeDtypeStruct((8, 2 * ROWS), bf16),
        ),
        in_specs=[vmem] * 4,
        out_specs=(anywhere,) * 4,
        scratch_shapes=[pltpu.VMEM((8, 2 * ROWS), bf16), pltpu.SemaphoreType.DMA((4,))],
        compiler_params=pltpu.CompilerParams(vmem_limit_bytes=8 << 20),
        cost_estimate=pl.CostEstimate(flops=0, bytes_accessed=8 << 20, transcendentals=0),
    )(*results)


def solution(mesh):
    placed = (
        P("fsdp", "tp"),
        P("fsdp", None),
        P("fsdp", "tp"),
        P("fsdp", "tp"),
        P("fsdp", "tp"),
        P("fsdp", "tp"),
        P("fsdp", "tp"),
        P("fsdp", "tp"),
        P("fsdp", "tp", None, None),
        P("fsdp", "tp", None, None),
        P("fsdp"),
    )
    return jax.shard_map(
        shards,
        mesh=mesh,
        in_specs=placed,
        out_specs=(P("fsdp", "tp"), P("fsdp", "tp"), P("fsdp", "tp"), P("fsdp", "tp")),
        check_vma=False,
    )
```

```python
import jax
import jax.numpy as jnp
from jax import lax
from jax.experimental import pallas as pl
from jax.experimental.pallas import tpu as pltpu
from jax.sharding import PartitionSpec as P

MESH = pl.DeviceIdType.MESH
HEAD_SIZE = 128
CACHE_SLOTS = 1024
TOKENS = 16384

beta_one = 0.9
beta_two = 0.95
learn_rate = 0.003
weight_decay = 0.1
adam_eps = 1e-08
bias_one = 1.0 - 0.9**10
bias_two = 1.0 - 0.95**10

NX, NZ = 2, 4
ROWS = 320
COLS = 1024
HALF = COLS // 2
EARLY = 256
PADDED = 384
ORDER = ((1, 2), (1, 1), (1, 3), (0, 2), (0, 1), (0, 3), (1, 0), (0, 0))
SLABS = len(ORDER)
SLOT = {place: slot for slot, place in enumerate(ORDER)}
STREAMS = (
    ((1, 112, 144, 80), (0, 112, 144, 80), (0, 0, 112, 48)),
    ((1, 288, 32, 16), (0, 288, 32, 16), (0, 256, 32, 16)),
)
Z_TOTAL = sum(chunk[0][2] for chunk in STREAMS)
X_TOTAL = sum(chunk[2][2] for chunk in STREAMS)
Z_BEGIN = (0, STREAMS[0][0][2])
X_BEGIN = (0, STREAMS[0][2][2])


def kernel(
    attn_hbm,
    grad_hbm,
    master_hbm,
    one_hbm,
    two_hbm,
    query_hbm,
    new_key_hbm,
    new_value_hbm,
    keys_hbm,
    values_hbm,
    lengths_hbm,
    master_out,
    one_out,
    two_out,
    decoded_out,
    attn,
    grads,
    part,
    from_core,
    from_x,
    from_x_last,
    zo_near,
    zo_far,
    zs_near,
    zs_far,
    xs_near,
    xs_far,
    state,
    query,
    new_key,
    new_value,
    caches,
    lengths,
    weights,
    heads,
    mixed,
    fresh,
    attended,
    shares,
    arrived,
    totals,
    decoded,
    late_shares,
    late_arrived,
    load_sem,
    attn_sem,
    grad_sem,
    core_sem,
    x_sem,
    z_sem,
    attend_sem,
    share_sem,
    late_sem,
    send_sem,
    news_sem,
):
    f = lax.axis_index("fsdp")
    t = lax.axis_index("tp")
    x, z, k = f // (2 * NZ), lax.rem(f // 2, NZ), lax.rem(f, 2)
    y, x_hi = t // 2, lax.rem(t, 2)
    z_summed = lax.rem(z + 2 + y - f // 4 + 8, NZ)

    def chip(dx, dz):
        return lax.rem(x + dx, NX) * NZ + lax.rem(z + dz, NZ)

    def at(dx, dz, core):
        return (chip(dx, dz) * 2 + core, t)

    other_core = at(0, 0, 1 - k)
    other_x = at(1, 0, k)
    up, down = at(0, 1, k), at(0, 3, k)
    own = pl.multiple_of(k * ROWS, 64)
    given = pl.multiple_of((1 - k) * ROWS, 64)

    attn_loads = [
        pltpu.make_async_copy(
            attn_hbm.at[:, pl.ds(HALF * half, HALF)], attn.at[:, pl.ds(HALF * half, HALF)], attn_sem.at[half]
        )
        for half in range(2)
    ]
    grad_loads = []
    for slot, (dx, dz) in enumerate(ORDER):
        columns = pl.ds(pl.multiple_of(chip(dx, dz) * 2 * ROWS, 128), 2 * ROWS)
        grad_loads.append(
            pltpu.make_async_copy(grad_hbm.at[:, columns], grads.at[slot], grad_sem.at[slot])
        )
    late_loads = [
        pltpu.make_async_copy(src, dst, load_sem.at[n])
        for n, (src, dst) in enumerate(
            (
                (query_hbm, query),
                (new_key_hbm, new_key),
                (new_value_hbm, new_value),
                (lengths_hbm, lengths),
            )
        )
    ]
    late_loads += [
        pltpu.make_async_copy(keys_hbm, caches.at[0], load_sem.at[4]),
        pltpu.make_async_copy(values_hbm, caches.at[1], load_sem.at[4]),
        pltpu.make_async_copy(master_hbm, state.at[0], load_sem.at[5]),
        pltpu.make_async_copy(one_hbm, state.at[1], load_sem.at[5]),
        pltpu.make_async_copy(two_hbm, state.at[2], load_sem.at[5]),
    ]
    first_columns = pl.ds(pl.multiple_of(chip(*ORDER[0]) * 2 * ROWS, 128), 2 * ROWS)
    for piece in range(4):
        rows = pl.ds(256 * piece, 256)
        pltpu.make_async_copy(
            grad_hbm.at[rows, first_columns], grads.at[0, rows], grad_sem.at[0]
        ).start()
        pltpu.make_async_copy(
            attn_hbm.at[rows, pl.ds(0, HALF)], attn.at[rows, pl.ds(0, HALF)], attn_sem.at[0]
        ).start()

    barrier = pltpu.get_barrier_semaphore()
    up_y = (f, lax.rem(y + 1, 4) * 2 + x_hi)
    down_y = (f, lax.rem(y + 3, 4) * 2 + x_hi)
    across_x = (chip(1, 0) * 2 + k, y * 2 + 1 - x_hi)
    neighbours = (other_core, other_x, up, down, up_y, down_y, across_x)
    for device in neighbours:
        pl.semaphore_signal(barrier, inc=1, device_id=device, device_id_type=MESH)
    stays = t == f // 2

    def tell(n, *devices):
        for device in devices:
            pl.semaphore_signal(news_sem.at[n], inc=1, device_id=device, device_id_type=MESH)

    attn_loads[1].start()

    def remote(src, dst, send, recv, device):
        return pltpu.make_async_remote_copy(
            src_ref=src, dst_ref=dst, send_sem=send, recv_sem=recv, device_id=device, device_id_type=MESH
        )

    def wait_bytes(ref, sem):
        pltpu.make_async_copy(ref, ref, sem).wait()

    def core_copy(slot):
        return remote(
            part.at[slot, pl.ds(given, ROWS)],
            from_core.at[slot],
            send_sem.at[0],
            core_sem.at[slot],
            other_core,
        )

    def own_rows(dx, dz, first, count):
        rows = pl.ds(pl.multiple_of(own + first, 16), count)
        return part.at[SLOT[dx, dz], rows]

    def add_own(dx, dz, first, count, *terms):
        ref = own_rows(dx, dz, first, count)
        for begin in range(0, count, 16):
            rows = pl.ds(begin, 16)
            total = ref[rows, :]
            for term in terms:
                total = total + term[rows, :]
            ref[rows, :] = total

    def x_landing(chunk, dz):
        return from_x.at[dz, pl.ds(X_BEGIN[chunk], STREAMS[chunk][2][2])]

    def x_copy(chunk, dz):
        _, first, count, _ = STREAMS[chunk][2]
        return remote(
            own_rows(1, dz, first, count),
            x_landing(chunk, dz),
            send_sem.at[1],
            x_sem.at[chunk, dz],
            other_x,
        )

    over_x = [[x_copy(chunk, dz) for dz in range(NZ)] for chunk in range(2)]

    def z_landing(chunk):
        return from_x_last.at[pl.ds(Z_BEGIN[chunk], STREAMS[chunk][0][2])]

    def last_copy(chunk):
        _, first, count, _ = STREAMS[chunk][0]
        return remote(
            own_rows(1, 0, first, count),
            z_landing(chunk),
            send_sem.at[2],
            x_sem.at[chunk, NZ],
            other_x,
        )

    last_x = [last_copy(chunk) for chunk in range(2)]

    class Stream:
        def __init__(self, chunk, number, near, far):
            dx, first, count, cut = STREAMS[chunk][number]
            rest = count - cut
            place = pl.ds((X_BEGIN if number == 2 else Z_BEGIN)[chunk], count)
            self.dx, self.first, self.count, self.cut, self.rest = dx, first, count, cut, rest
            self.near, self.far = near.at[:, place], far.at[place]

            def send(dz, begin, size, dst, n, device):
                return remote(
                    own_rows(dx, dz, first + begin, size),
                    dst,
                    send_sem.at[3 + 2 * number + n // 2],
                    z_sem.at[chunk, number, n],
                    device,
                )

            near, far = self.near, self.far
            self.far_up = send(2, 0, cut, far.at[pl.ds(0, cut)], 0, up)
            self.far_down = send(2, cut, rest, far.at[pl.ds(cut, rest)], 1, down)
            self.up_free = send(1, cut, rest, near.at[0, pl.ds(cut, rest)], 2, up)
            self.up_late = send(1, 0, cut, near.at[0, pl.ds(0, cut)], 2, up)
            self.down_free = send(3, 0, cut, near.at[1, pl.ds(0, cut)], 2, down)
            self.down_late = send(3, cut, rest, near.at[1, pl.ds(cut, rest)], 2, down)
            self.near_sem = z_sem.at[chunk, number, 2]

        def start_far(self):
            self.far_up.start()
            self.far_down.start()

        def start_free(self):
            self.up_free.start()
            self.down_free.start()

        def pass_far(self):
            self.far_up.wait_recv()
            add_own(self.dx, 1, self.first, self.cut, self.far.at[pl.ds(0, self.cut)])
            self.up_late.start()
            self.far_down.wait_recv()
            add_own(self.dx, 3, self.first + self.cut, self.rest, self.far.at[pl.ds(self.cut, self.rest)])
            self.down_late.start()

        def wait_near(self):
            wait_bytes(self.near, self.near_sem)

    zo = [Stream(chunk, 0, zo_near, zo_far) for chunk in range(2)]
    zs = [Stream(chunk, 1, zs_near, zs_far) for chunk in range(2)]
    xs = [Stream(chunk, 2, xs_near, xs_far) for chunk in range(2)]

    def add_x(chunk, dz):
        over_x[chunk][dz].wait_recv()
        _, first, count, _ = STREAMS[chunk][2]
        add_own(0, dz, first, count, x_landing(chunk, dz))

    def x_far(chunk):
        add_x(chunk, 2)
        xs[chunk].start_far()

    def x_up(chunk):
        add_x(chunk, 1)
        xs[chunk].up_free.start()

    def x_down(chunk):
        add_x(chunk, 3)
        xs[chunk].down_free.start()

    def send_last(chunk, start=True):
        stream = zo[chunk]
        stream.wait_near()
        add_own(1, 0, stream.first, stream.count, stream.near.at[0], stream.near.at[1])
        if start:
            last_x[chunk].start()

    def split_heads():
        for copy in late_loads[:4]:
            copy.wait()
        wait_bytes(caches, load_sem.at[4])
        for head in range(8):
            heads[pl.ds(8 * head, 8), :] = query[:, pl.ds(HEAD_SIZE * head, HEAD_SIZE)].astype(jnp.float32)
        fresh[0] = new_key[...].astype(jnp.float32)
        fresh[1] = new_value[...].astype(jnp.float32)

    score_scale = 1.0 / HEAD_SIZE**0.5

    def attend(row):
        own_heads = heads[pl.ds(row, 8, stride=8), :]
        scores = (
            lax.dot_general(
                own_heads.astype(jnp.bfloat16),
                caches[0, row, 0],
                (((1,), (1,)), ((), ())),
                preferred_element_type=jnp.float32,
            )
            * score_scale
        )
        slots = lax.broadcasted_iota(jnp.int32, (8, CACHE_SLOTS), 1)
        scores = jnp.where(slots < lengths[row], scores, -jnp.inf)
        new_score = (
            jnp.sum(own_heads * fresh[0, pl.ds(row, 1), :], axis=-1, keepdims=True) * score_scale
        )
        top = jnp.maximum(jnp.max(scores, axis=-1, keepdims=True), new_score)
        expo = jnp.exp(scores - top)
        expo_new = jnp.exp(new_score - top)
        total = jnp.sum(expo, axis=-1, keepdims=True) + expo_new
        probs = (expo / total).astype(jnp.bfloat16)
        prob_new = (expo_new / total).astype(jnp.bfloat16).astype(jnp.float32)
        mixed[pl.ds(row, 8, stride=8), :] = (
            jnp.dot(probs, caches[1, row, 0], preferred_element_type=jnp.float32)
            + prob_new * fresh[1, pl.ds(row, 1), :]
        )

    here = chip(0, 0)
    gathers = [
        remote(
            attended.at[k, here],
            attended.at[k, here],
            attend_sem.at[0],
            attend_sem.at[1],
            at(place // NZ, place % NZ, k),
        )
        for place in range(1, NX * NZ)
    ]
    swap = remote(
        attended.at[k], attended.at[k], attend_sem.at[2], attend_sem.at[3], other_core
    )

    def send_attended():
        halves = [
            jnp.concatenate(
                [mixed[pl.ds(8 * head, 8), :] for head in range(4 * half, 4 * half + 4)], axis=1
            )
            for half in range(2)
        ]
        attended[k, here] = jnp.concatenate(halves, axis=0).astype(jnp.bfloat16)
        for copy in gathers:
            copy.start()

    after = (
        None,
        (over_x[0][1].start, zo[0].up_free.start, over_x[1][1].start, zo[1].up_free.start, split_heads),
        (over_x[0][3].start, zo[0].down_free.start, zo[1].down_free.start, zo[0].pass_far),
        (zs[0].start_far, zo[1].pass_far, lambda: x_far(0)),
        (zs[0].up_free.start,),
        (zs[0].down_free.start, lambda: x_up(0)),
        (lambda: send_last(0, False), send_attended, over_x[0][0].start, last_x[0].start),
        (),
    )
    first_row = 3

    def first_core_copy(half):
        columns = pl.ds(HALF * half, HALF)
        return remote(
            part.at[0, pl.ds(given, ROWS), columns],
            from_core.at[0, :, columns],
            send_sem.at[0],
            core_sem.at[SLABS * half],
            other_core,
        )

    def slab_half(slot, half, rows):
        columns = pl.ds(HALF * half, HALF)
        part[slot, rows, columns] = lax.dot_general(
            grads[slot, :, rows], attn[:, columns], (((0,), (0,)), ((), ())), preferred_element_type=jnp.float32
        ).astype(jnp.bfloat16)

    def send_first(half):
        columns = pl.ds(HALF * half, HALF)
        first_core_copy(half).wait_recv()
        for begin in range(0, ROWS, 16):
            rows = pl.ds(pl.multiple_of(own + begin, 16), 16)
            part[0, rows, columns] = part[0, rows, columns] + from_core[0, pl.ds(begin, 16), columns]
        _, first, count, _ = STREAMS[0][2]
        remote(
            own_rows(1, 2, first, count).at[:, columns],
            x_landing(0, 2).at[:, columns],
            send_sem.at[1],
            x_sem.at[0, 2],
            other_x,
        ).start()
        _, first, count, cut = STREAMS[0][0]
        for n, begin, size, device in ((0, 0, cut, up), (1, cut, count - cut, down)):
            remote(
                own_rows(1, 2, first + begin, size).at[:, columns],
                zo[0].far.at[pl.ds(begin, size), columns],
                send_sem.at[3],
                z_sem.at[0, 0, n],
                device,
            ).start()

    grad_loads[0].wait()
    for half in range(2):
        attn_loads[half].wait()
        slab_half(0, half, pl.ds(pl.multiple_of((1 - k) * 256, 128), 384))
        if half == 0:
            pl.semaphore_wait(barrier, len(neighbours))
            grad_loads[1].start()
        first_core_copy(half).start()
        slab_half(0, half, pl.ds(pl.multiple_of(k * 384, 128), 256))
    grad_loads[2].start()
    for copy in late_loads[:6]:
        copy.start()
    send_first(0)
    grad_loads[1].wait()
    slab_half(1, 0, pl.ds(0, 2 * ROWS))
    send_first(1)
    over_x[1][2].start()
    zo[1].start_far()
    slab_half(1, 1, pl.ds(0, 2 * ROWS))
    core_copy(1).start()
    grad_loads[3].start()

    @pl.loop(2, SLABS + 1)
    def _(step):
        @pl.when(step < SLABS)
        def _():
            pltpu.make_async_copy(
                grad_hbm.at[:, pl.ds(0, 2 * ROWS)], grads.at[step], grad_sem.at[step]
            ).wait()

        for slot in range(4, SLABS):
            @pl.when(step == slot - 2)
            def _():
                grad_loads[slot].start()
                if slot == 6:
                    for copy in late_loads[6:]:
                        copy.start()

        @pl.when(step < SLABS)
        def _():
            part[step] = lax.dot_general(
                grads[step], attn[...], (((0,), (0,)), ((), ())), preferred_element_type=jnp.float32
            ).astype(jnp.bfloat16)
            core_copy(step).start()

        done = step - 1
        core_copy(done).wait_recv()
        rows = pl.ds(own, ROWS)
        part[done, rows, :] = part[done, rows, :] + from_core[done]

        for slot in range(1, SLABS):
            @pl.when(step == slot + 1)
            def _():
                for action in after[slot]:
                    action()

        @pl.when(jnp.logical_and(step >= first_row, step < first_row + 4))
        def _():
            attend(2 * (step - first_row))
            attend(2 * (step - first_row) + 1)

    tell(0, up_y, down_y)
    zs[0].pass_far()
    x_down(0)
    xs[0].pass_far()
    zs[1].start_far()
    x_far(1)
    zs[1].start_free()
    x_up(1)
    over_x[1][3].start()
    over_x[1][0].start()
    send_last(1)
    pl.semaphore_wait(news_sem.at[0], 2)
    tell(1, up_y, down_y)
    wait_bytes(attended.at[k, pl.ds(0, 7)], attend_sem.at[1])
    swap.start()
    pl.semaphore_wait(news_sem.at[1], 2)
    tell(2, across_x)
    weights[pl.ds(ROWS, PADDED - ROWS), :] = jnp.zeros((PADDED - ROWS, COLS), jnp.bfloat16)
    wait_bytes(state, load_sem.at[5])

    def adam(first, count, terms):
        @pl.loop(0, count // 16)
        def _(n):
            begin = pl.multiple_of(n * 16, 16)
            rows = pl.ds(pl.multiple_of(first + begin, 16), 16)
            mine = pl.ds(pl.multiple_of(own + first + begin, 16), 16)
            total = part[SLOT[0, 0], mine, :].astype(jnp.float32)
            for term in terms:
                total = total + term[pl.ds(begin, 16), :].astype(jnp.float32)
            grad = total * (1.0 / TOKENS)
            one_new = beta_one * state[1, rows, :] + (1.0 - beta_one) * grad
            two_new = beta_two * state[2, rows, :] + (1.0 - beta_two) * grad * grad
            update = (one_new * (1.0 / bias_one)) / (jnp.sqrt(two_new * (1.0 / bias_two)) + adam_eps)
            master_new = state[0, rows, :] * (1.0 - learn_rate * weight_decay) - learn_rate * update
            one_out[rows, :] = one_new
            two_out[rows, :] = two_new
            master_out[rows, :] = master_new
            weights[rows, :] = master_new.astype(jnp.bfloat16)

    def adam_x(chunk):
        xs[chunk].wait_near()
        over_x[chunk][0].wait_recv()
        _, first, count, _ = STREAMS[chunk][2]
        adam(first, count, (x_landing(chunk, 0), xs[chunk].near.at[0], xs[chunk].near.at[1]))

    def adam_z(chunk):
        zs[chunk].wait_near()
        last_x[chunk].wait_recv()
        _, first, count, _ = STREAMS[chunk][1]
        adam(first, count, (z_landing(chunk), zs[chunk].near.at[0], zs[chunk].near.at[1]))

    def product(first, count):
        halves = [
            lax.dot_general(
                attended[...].reshape(256, HALF),
                weights[pl.ds(first, count), pl.ds(HALF * half, HALF)],
                (((1,), (1,)), ((), ())),
                preferred_element_type=jnp.float32,
            ).reshape(2, 8, 16, count)[:, :, 8 * half : 8 * half + 8, :]
            for half in range(2)
        ]
        return halves[0] + halves[1]

    adam_z(0)
    adam_x(0)
    swap.wait_recv()
    share = product(0, EARLY)
    pl.semaphore_wait(news_sem.at[2], 1)
    for place in range(NZ):
        shares[place] = jnp.concatenate(
            [share[core, dx * NZ + place] for dx in range(NX) for core in range(2)], axis=0
        ).astype(jnp.bfloat16)

    for step in (2, 1, 3):
        remote(
            shares.at[lax.rem(z_summed + step, NZ)],
            arrived.at[step - 1],
            share_sem.at[0],
            share_sem.at[1],
            (f, lax.rem(y + step, 4) * 2 + x_hi),
        ).start()

    zs[1].pass_far()
    x_down(1)
    xs[1].pass_far()
    adam_z(1)
    adam_x(1)
    late_shares[...] = product(EARLY, PADDED - EARLY).reshape(16, 8, PADDED - EARLY)

    def late_copy(step):
        target = lax.rem(f + step, 16)
        return remote(
            late_shares.at[lax.rem(target, 2) * 8 + target // 2],
            late_arrived.at[k, t],
            late_sem.at[0],
            late_sem.at[1],
            (target, f // 2),
        )

    for step in range(1, 16):
        late_copy(step).start()

    @pl.when(stays)
    def _():
        pltpu.make_async_copy(
            late_shares.at[k * 8 + f // 2], late_arrived.at[k, t], late_sem.at[1]
        ).start()

    @pl.when(jnp.logical_not(stays))
    def _():
        late_copy(0).start()

    wait_bytes(arrived, share_sem.at[1])
    total = shares[z_summed].astype(jnp.float32)
    for step in range(3):
        total = total + arrived[step].astype(jnp.float32)
    totals[...] = total
    for dx in range(NX):
        for core in range(2):
            remote(
                totals.at[pl.ds(8 * (2 * dx + core), 8)],
                decoded.at[k, x_hi],
                share_sem.at[2],
                share_sem.at[3],
                ((dx * NZ + z_summed) * 2 + core, f // 2),
            ).start()

    wait_bytes(from_core, send_sem.at[0])
    wait_bytes(from_x, send_sem.at[1])
    wait_bytes(from_x_last, send_sem.at[2])
    for number, (near, far) in enumerate(((zo_near, zo_far), (zs_near, zs_far), (xs_near, xs_far))):
        wait_bytes(far, send_sem.at[3 + 2 * number])
        wait_bytes(near, send_sem.at[4 + 2 * number])
    wait_bytes(attended.at[k, pl.ds(0, 7)], attend_sem.at[0])
    swap.wait_send()
    wait_bytes(arrived, share_sem.at[0])
    wait_bytes(decoded, share_sem.at[2])

    @pl.when(stays)
    def _():
        wait_bytes(late_shares.at[pl.ds(0, 15)], late_sem.at[0])

    @pl.when(jnp.logical_not(stays))
    def _():
        wait_bytes(late_shares, late_sem.at[0])

    wait_bytes(decoded, share_sem.at[3])
    decoded_out[:, :, pl.ds(0, EARLY)] = decoded[:, 0] + decoded[:, 1]
    wait_bytes(late_arrived, late_sem.at[1])
    decoded_out[:, :, pl.ds(EARLY, PADDED - EARLY)] = jnp.sum(late_arrived[...], axis=1)


def write_kernel(master, one, two, decoded, master_out, one_out, two_out, decoded_out, rounded, sems):
    pairs = ((master, master_out), (one, one_out), (two, two_out))
    for piece in range(4):
        rows = pl.ds(ROWS // 4 * piece, ROWS // 4)
        for n, (src, dst) in enumerate(pairs):
            pltpu.make_async_copy(src.at[rows], dst.at[rows], sems.at[n]).start()
    rounded[...] = jnp.concatenate(
        [decoded[core, :, :ROWS] for core in range(2)], axis=1
    ).astype(jnp.bfloat16)
    last = pltpu.make_async_copy(rounded, decoded_out, sems.at[3])
    last.start()
    for n, (src, dst) in enumerate(pairs):
        pltpu.make_async_copy(src, dst, sems.at[n]).wait()
    last.wait()


def shards(*args):
    bf16, f32 = jnp.bfloat16, jnp.float32
    vmem = pl.BlockSpec(memory_space=pltpu.VMEM)
    anywhere = pl.BlockSpec(memory_space=pl.ANY)
    results = pl.pallas_call(
        kernel,
        out_shape=(
            pltpu.VMEM((ROWS, COLS), f32),
            pltpu.VMEM((ROWS, COLS), f32),
            pltpu.VMEM((ROWS, COLS), f32),
            pltpu.VMEM((2, 8, PADDED), f32),
        ),
        in_specs=[anywhere] * 11,
        out_specs=(vmem,) * 4,
        scratch_shapes=[
            pltpu.VMEM((1024, COLS), bf16),
            pltpu.VMEM((SLABS, 1024, 2 * ROWS), bf16),
            pltpu.VMEM((SLABS, 2 * ROWS, COLS), bf16),
            pltpu.VMEM((SLABS, ROWS, COLS), bf16),
            pltpu.VMEM((NZ, X_TOTAL, COLS), bf16),
            pltpu.VMEM((Z_TOTAL, COLS), bf16),
            pltpu.VMEM((2, Z_TOTAL, COLS), bf16),
            pltpu.VMEM((Z_TOTAL, COLS), bf16),
            pltpu.VMEM((2, Z_TOTAL, COLS), bf16),
            pltpu.VMEM((Z_TOTAL, COLS), bf16),
            pltpu.VMEM((2, X_TOTAL, COLS), bf16),
            pltpu.VMEM((X_TOTAL, COLS), bf16),
            pltpu.VMEM((3, ROWS, COLS), f32),
            pltpu.VMEM((8, 1024), bf16),
            pltpu.VMEM((8, HEAD_SIZE), bf16),
            pltpu.VMEM((8, HEAD_SIZE), bf16),
            pltpu.VMEM((2, 8, 1, CACHE_SLOTS, HEAD_SIZE), bf16),
            pltpu.SMEM((8,), jnp.int32),
            pltpu.VMEM((PADDED, COLS), bf16),
            pltpu.VMEM((64, HEAD_SIZE), f32),
            pltpu.VMEM((64, HEAD_SIZE), f32),
            pltpu.VMEM((2, 8, HEAD_SIZE), f32),
            pltpu.VMEM((2, 8, 16, HALF), bf16),
            pltpu.VMEM((NZ, 32, EARLY), bf16),
            pltpu.VMEM((3, 32, EARLY), bf16),
            pltpu.VMEM((32, EARLY), f32),
            pltpu.VMEM((2, 2, 8, EARLY), f32),
            pltpu.VMEM((16, 8, PADDED - EARLY), f32),
            pltpu.VMEM((2, 8, 8, PADDED - EARLY), f32),
            pltpu.SemaphoreType.DMA((6,)),
            pltpu.SemaphoreType.DMA((2,)),
            pltpu.SemaphoreType.DMA((SLABS,)),
            pltpu.SemaphoreType.DMA((SLABS + 1,)),
            pltpu.SemaphoreType.DMA((2, NZ + 1)),
            pltpu.SemaphoreType.DMA((2, 3, 3)),
            pltpu.SemaphoreType.DMA((4,)),
            pltpu.SemaphoreType.DMA((4,)),
            pltpu.SemaphoreType.DMA((2,)),
            pltpu.SemaphoreType.DMA((9,)),
            pltpu.SemaphoreType.REGULAR((3,)),
        ],
        compiler_params=pltpu.CompilerParams(
            collective_id=0, has_side_effects=True, vmem_limit_bytes=50 << 20
        ),
        cost_estimate=pl.CostEstimate(
            flops=2 * 1024 * 1024 * 5120, bytes_accessed=24 << 20, transcendentals=1 << 19
        ),
    )(*(pltpu.with_memory_space_constraint(arg, pltpu.HBM) for arg in args))
    return pl.pallas_call(
        write_kernel,
        out_shape=(
            jax.ShapeDtypeStruct((ROWS, COLS), f32),
            jax.ShapeDtypeStruct((ROWS, COLS), f32),
            jax.ShapeDtypeStruct((ROWS, COLS), f32),
            jax.ShapeDtypeStruct((8, 2 * ROWS), bf16),
        ),
        in_specs=[vmem] * 4,
        out_specs=(anywhere,) * 4,
        scratch_shapes=[pltpu.VMEM((8, 2 * ROWS), bf16), pltpu.SemaphoreType.DMA((4,))],
        compiler_params=pltpu.CompilerParams(vmem_limit_bytes=8 << 20),
        cost_estimate=pl.CostEstimate(flops=0, bytes_accessed=8 << 20, transcendentals=0),
    )(*results)


def solution(mesh):
    placed = (
        P("fsdp", "tp"),
        P("fsdp", None),
        P("fsdp", "tp"),
        P("fsdp", "tp"),
        P("fsdp", "tp"),
        P("fsdp", "tp"),
        P("fsdp", "tp"),
        P("fsdp", "tp"),
        P("fsdp", "tp", None, None),
        P("fsdp", "tp", None, None),
        P("fsdp"),
    )
    return jax.shard_map(
        shards,
        mesh=mesh,
        in_specs=placed,
        out_specs=(P("fsdp", "tp"), P("fsdp", "tp"), P("fsdp", "tp"), P("fsdp", "tp")),
        check_vma=False,
    )
```

```python
import jax
import jax.numpy as jnp
from jax import lax
from jax.experimental import pallas as pl
from jax.experimental.pallas import tpu as pltpu
from jax.sharding import PartitionSpec as P

MESH = pl.DeviceIdType.MESH
HEAD_SIZE = 128
CACHE_SLOTS = 1024
TOKENS = 16384

beta_one = 0.9
beta_two = 0.95
learn_rate = 0.003
weight_decay = 0.1
adam_eps = 1e-08
bias_one = 1.0 - 0.9**10
bias_two = 1.0 - 0.95**10

NX, NZ = 2, 4
ROWS = 320
COLS = 1024
HALF = COLS // 2
EARLY = 256
PADDED = 384
ORDER = ((1, 2), (1, 1), (1, 3), (0, 2), (0, 1), (0, 3), (1, 0), (0, 0))
SLABS = len(ORDER)
SLOT = {place: slot for slot, place in enumerate(ORDER)}
STREAMS = (
    ((1, 112, 144, 80), (0, 112, 144, 80), (0, 0, 112, 48)),
    ((1, 288, 32, 16), (0, 288, 32, 16), (0, 256, 32, 16)),
)
Z_TOTAL = sum(chunk[0][2] for chunk in STREAMS)
X_TOTAL = sum(chunk[2][2] for chunk in STREAMS)
Z_BEGIN = (0, STREAMS[0][0][2])
X_BEGIN = (0, STREAMS[0][2][2])


def kernel(
    attn_hbm,
    grad_hbm,
    master_hbm,
    one_hbm,
    two_hbm,
    query_hbm,
    new_key_hbm,
    new_value_hbm,
    keys_hbm,
    values_hbm,
    lengths_hbm,
    master_out,
    one_out,
    two_out,
    decoded_out,
    attn,
    grads,
    part,
    from_core,
    from_x,
    from_x_last,
    zo_near,
    zo_far,
    zs_near,
    zs_far,
    xs_near,
    xs_far,
    state,
    query,
    new_key,
    new_value,
    caches,
    lengths,
    weights,
    heads,
    mixed,
    fresh,
    attended,
    shares,
    arrived,
    totals,
    decoded,
    late_shares,
    late_arrived,
    load_sem,
    attn_sem,
    grad_sem,
    core_sem,
    x_sem,
    z_sem,
    attend_sem,
    share_sem,
    late_sem,
    send_sem,
    news_sem,
):
    f = lax.axis_index("fsdp")
    t = lax.axis_index("tp")
    x, z, k = f // (2 * NZ), lax.rem(f // 2, NZ), lax.rem(f, 2)
    y, x_hi = t // 2, lax.rem(t, 2)
    z_summed = lax.rem(z + 2 + y - f // 4 + 8, NZ)

    def chip(dx, dz):
        return lax.rem(x + dx, NX) * NZ + lax.rem(z + dz, NZ)

    def at(dx, dz, core):
        return (chip(dx, dz) * 2 + core, t)

    other_core = at(0, 0, 1 - k)
    other_x = at(1, 0, k)
    up, down = at(0, 1, k), at(0, 3, k)
    own = pl.multiple_of(k * ROWS, 64)
    given = pl.multiple_of((1 - k) * ROWS, 64)

    attn_loads = [
        pltpu.make_async_copy(
            attn_hbm.at[:, pl.ds(HALF * half, HALF)], attn.at[:, pl.ds(HALF * half, HALF)], attn_sem.at[half]
        )
        for half in range(2)
    ]
    grad_loads = []
    for slot, (dx, dz) in enumerate(ORDER):
        columns = pl.ds(pl.multiple_of(chip(dx, dz) * 2 * ROWS, 128), 2 * ROWS)
        grad_loads.append(
            pltpu.make_async_copy(grad_hbm.at[:, columns], grads.at[slot], grad_sem.at[slot])
        )
    late_loads = [
        pltpu.make_async_copy(src, dst, load_sem.at[n])
        for n, (src, dst) in enumerate(
            (
                (query_hbm, query),
                (new_key_hbm, new_key),
                (new_value_hbm, new_value),
                (lengths_hbm, lengths),
            )
        )
    ]
    late_loads += [
        pltpu.make_async_copy(keys_hbm, caches.at[0], load_sem.at[4]),
        pltpu.make_async_copy(values_hbm, caches.at[1], load_sem.at[4]),
        pltpu.make_async_copy(master_hbm, state.at[0], load_sem.at[5]),
        pltpu.make_async_copy(one_hbm, state.at[1], load_sem.at[5]),
        pltpu.make_async_copy(two_hbm, state.at[2], load_sem.at[5]),
    ]
    first_columns = pl.ds(pl.multiple_of(chip(*ORDER[0]) * 2 * ROWS, 128), 2 * ROWS)
    for piece in range(4):
        rows = pl.ds(256 * piece, 256)
        pltpu.make_async_copy(
            grad_hbm.at[rows, first_columns], grads.at[0, rows], grad_sem.at[0]
        ).start()
        pltpu.make_async_copy(
            attn_hbm.at[rows, pl.ds(0, HALF)], attn.at[rows, pl.ds(0, HALF)], attn_sem.at[0]
        ).start()

    barrier = pltpu.get_barrier_semaphore()
    up_y = (f, lax.rem(y + 1, 4) * 2 + x_hi)
    down_y = (f, lax.rem(y + 3, 4) * 2 + x_hi)
    across_x = (chip(1, 0) * 2 + k, y * 2 + 1 - x_hi)
    neighbours = (other_core, other_x, up, down, up_y, down_y, across_x)
    for device in neighbours:
        pl.semaphore_signal(barrier, inc=1, device_id=device, device_id_type=MESH)
    stays = t == f // 2

    def tell(n, *devices):
        for device in devices:
            pl.semaphore_signal(news_sem.at[n], inc=1, device_id=device, device_id_type=MESH)

    attn_loads[1].start()

    def remote(src, dst, send, recv, device):
        return pltpu.make_async_remote_copy(
            src_ref=src, dst_ref=dst, send_sem=send, recv_sem=recv, device_id=device, device_id_type=MESH
        )

    def wait_bytes(ref, sem):
        pltpu.make_async_copy(ref, ref, sem).wait()

    def core_copy(slot):
        return remote(
            part.at[slot, pl.ds(given, ROWS)],
            from_core.at[slot],
            send_sem.at[0],
            core_sem.at[slot],
            other_core,
        )

    def own_rows(dx, dz, first, count):
        rows = pl.ds(pl.multiple_of(own + first, 16), count)
        return part.at[SLOT[dx, dz], rows]

    def add_own(dx, dz, first, count, *terms):
        ref = own_rows(dx, dz, first, count)
        for begin in range(0, count, 16):
            rows = pl.ds(begin, 16)
            total = ref[rows, :]
            for term in terms:
                total = total + term[rows, :]
            ref[rows, :] = total

    def x_landing(chunk, dz):
        return from_x.at[dz, pl.ds(X_BEGIN[chunk], STREAMS[chunk][2][2])]

    def x_copy(chunk, dz):
        _, first, count, _ = STREAMS[chunk][2]
        return remote(
            own_rows(1, dz, first, count),
            x_landing(chunk, dz),
            send_sem.at[1],
            x_sem.at[chunk, dz],
            other_x,
        )

    over_x = [[x_copy(chunk, dz) for dz in range(NZ)] for chunk in range(2)]

    def z_landing(chunk):
        return from_x_last.at[pl.ds(Z_BEGIN[chunk], STREAMS[chunk][0][2])]

    def last_copy(chunk):
        _, first, count, _ = STREAMS[chunk][0]
        return remote(
            own_rows(1, 0, first, count),
            z_landing(chunk),
            send_sem.at[2],
            x_sem.at[chunk, NZ],
            other_x,
        )

    last_x = [last_copy(chunk) for chunk in range(2)]

    class Stream:
        def __init__(self, chunk, number, near, far):
            dx, first, count, cut = STREAMS[chunk][number]
            rest = count - cut
            place = pl.ds((X_BEGIN if number == 2 else Z_BEGIN)[chunk], count)
            self.dx, self.first, self.count, self.cut, self.rest = dx, first, count, cut, rest
            self.near, self.far = near.at[:, place], far.at[place]

            def send(dz, begin, size, dst, n, device):
                return remote(
                    own_rows(dx, dz, first + begin, size),
                    dst,
                    send_sem.at[3 + 2 * number + n // 2],
                    z_sem.at[chunk, number, n],
                    device,
                )

            near, far = self.near, self.far
            self.far_up = send(2, 0, cut, far.at[pl.ds(0, cut)], 0, up)
            self.far_down = send(2, cut, rest, far.at[pl.ds(cut, rest)], 1, down)
            self.up_free = send(1, cut, rest, near.at[0, pl.ds(cut, rest)], 2, up)
            self.up_late = send(1, 0, cut, near.at[0, pl.ds(0, cut)], 2, up)
            self.down_free = send(3, 0, cut, near.at[1, pl.ds(0, cut)], 2, down)
            self.down_late = send(3, cut, rest, near.at[1, pl.ds(cut, rest)], 2, down)
            self.near_sem = z_sem.at[chunk, number, 2]

        def start_far(self):
            self.far_up.start()
            self.far_down.start()

        def start_free(self):
            self.up_free.start()
            self.down_free.start()

        def pass_far(self):
            self.far_up.wait_recv()
            add_own(self.dx, 1, self.first, self.cut, self.far.at[pl.ds(0, self.cut)])
            self.up_late.start()
            self.far_down.wait_recv()
            add_own(self.dx, 3, self.first + self.cut, self.rest, self.far.at[pl.ds(self.cut, self.rest)])
            self.down_late.start()

        def wait_near(self):
            wait_bytes(self.near, self.near_sem)

    zo = [Stream(chunk, 0, zo_near, zo_far) for chunk in range(2)]
    zs = [Stream(chunk, 1, zs_near, zs_far) for chunk in range(2)]
    xs = [Stream(chunk, 2, xs_near, xs_far) for chunk in range(2)]

    def add_x(chunk, dz):
        over_x[chunk][dz].wait_recv()
        _, first, count, _ = STREAMS[chunk][2]
        add_own(0, dz, first, count, x_landing(chunk, dz))

    def x_far(chunk):
        add_x(chunk, 2)
        xs[chunk].start_far()

    def x_up(chunk):
        add_x(chunk, 1)
        xs[chunk].up_free.start()

    def x_down(chunk):
        add_x(chunk, 3)
        xs[chunk].down_free.start()

    def send_last(chunk, start=True):
        stream = zo[chunk]
        stream.wait_near()
        add_own(1, 0, stream.first, stream.count, stream.near.at[0], stream.near.at[1])
        if start:
            last_x[chunk].start()

    def split_heads():
        for copy in late_loads[:4]:
            copy.wait()
        wait_bytes(caches, load_sem.at[4])
        for head in range(8):
            heads[pl.ds(8 * head, 8), :] = query[:, pl.ds(HEAD_SIZE * head, HEAD_SIZE)].astype(jnp.float32)
        fresh[0] = new_key[...].astype(jnp.float32)
        fresh[1] = new_value[...].astype(jnp.float32)

    score_scale = 1.0 / HEAD_SIZE**0.5

    def attend(row):
        own_heads = heads[pl.ds(row, 8, stride=8), :]
        scores = (
            lax.dot_general(
                own_heads.astype(jnp.bfloat16),
                caches[0, row, 0],
                (((1,), (1,)), ((), ())),
                preferred_element_type=jnp.float32,
            )
            * score_scale
        )
        slots = lax.broadcasted_iota(jnp.int32, (8, CACHE_SLOTS), 1)
        scores = jnp.where(slots < lengths[row], scores, -jnp.inf)
        new_score = (
            jnp.sum(own_heads * fresh[0, pl.ds(row, 1), :], axis=-1, keepdims=True) * score_scale
        )
        top = jnp.maximum(jnp.max(scores, axis=-1, keepdims=True), new_score)
        expo = jnp.exp(scores - top)
        expo_new = jnp.exp(new_score - top)
        total = jnp.sum(expo, axis=-1, keepdims=True) + expo_new
        probs = (expo / total).astype(jnp.bfloat16)
        prob_new = (expo_new / total).astype(jnp.bfloat16).astype(jnp.float32)
        mixed[pl.ds(row, 8, stride=8), :] = (
            jnp.dot(probs, caches[1, row, 0], preferred_element_type=jnp.float32)
            + prob_new * fresh[1, pl.ds(row, 1), :]
        )

    here = chip(0, 0)
    gathers = [
        remote(
            attended.at[k, here],
            attended.at[k, here],
            attend_sem.at[0],
            attend_sem.at[1],
            at(place // NZ, place % NZ, k),
        )
        for place in range(1, NX * NZ)
    ]
    swap = remote(
        attended.at[k], attended.at[k], attend_sem.at[2], attend_sem.at[3], other_core
    )

    def send_attended():
        halves = [
            jnp.concatenate(
                [mixed[pl.ds(8 * head, 8), :] for head in range(4 * half, 4 * half + 4)], axis=1
            )
            for half in range(2)
        ]
        attended[k, here] = jnp.concatenate(halves, axis=0).astype(jnp.bfloat16)
        for copy in gathers:
            copy.start()

    after = (
        None,
        (over_x[0][1].start, zo[0].up_free.start, over_x[1][1].start, zo[1].up_free.start, split_heads),
        (over_x[0][3].start, zo[0].down_free.start, zo[1].down_free.start, zo[0].pass_far),
        (zs[0].start_far, zo[1].pass_far, lambda: x_far(0)),
        (zs[0].up_free.start,),
        (zs[0].down_free.start, lambda: x_up(0)),
        (lambda: send_last(0, False), send_attended, over_x[0][0].start, last_x[0].start),
        (),
    )
    first_row = 3

    def first_core_copy(half):
        columns = pl.ds(HALF * half, HALF)
        return remote(
            part.at[0, pl.ds(given, ROWS), columns],
            from_core.at[0, :, columns],
            send_sem.at[0],
            core_sem.at[SLABS * half],
            other_core,
        )

    def slab_half(slot, half, rows):
        columns = pl.ds(HALF * half, HALF)
        part[slot, rows, columns] = lax.dot_general(
            grads[slot, :, rows], attn[:, columns], (((0,), (0,)), ((), ())), preferred_element_type=jnp.float32
        ).astype(jnp.bfloat16)

    def send_first(half):
        columns = pl.ds(HALF * half, HALF)
        first_core_copy(half).wait_recv()
        for begin in range(0, ROWS, 16):
            rows = pl.ds(pl.multiple_of(own + begin, 16), 16)
            part[0, rows, columns] = part[0, rows, columns] + from_core[0, pl.ds(begin, 16), columns]
        _, first, count, _ = STREAMS[0][2]
        remote(
            own_rows(1, 2, first, count).at[:, columns],
            x_landing(0, 2).at[:, columns],
            send_sem.at[1],
            x_sem.at[0, 2],
            other_x,
        ).start()
        _, first, count, cut = STREAMS[0][0]
        for n, begin, size, device in ((0, 0, cut, up), (1, cut, count - cut, down)):
            remote(
                own_rows(1, 2, first + begin, size).at[:, columns],
                zo[0].far.at[pl.ds(begin, size), columns],
                send_sem.at[3],
                z_sem.at[0, 0, n],
                device,
            ).start()

    grad_loads[0].wait()
    for half in range(2):
        attn_loads[half].wait()
        slab_half(0, half, pl.ds(pl.multiple_of((1 - k) * 256, 128), 384))
        if half == 0:
            pl.semaphore_wait(barrier, len(neighbours))
            grad_loads[1].start()
        first_core_copy(half).start()
        slab_half(0, half, pl.ds(pl.multiple_of(k * 384, 128), 256))
    grad_loads[2].start()
    for copy in late_loads[:6]:
        copy.start()
    send_first(0)
    grad_loads[1].wait()
    slab_half(1, 0, pl.ds(0, 2 * ROWS))
    send_first(1)
    over_x[1][2].start()
    zo[1].start_far()
    slab_half(1, 1, pl.ds(0, 2 * ROWS))
    core_copy(1).start()
    grad_loads[3].start()

    @pl.loop(2, SLABS + 1)
    def _(step):
        @pl.when(step < SLABS)
        def _():
            pltpu.make_async_copy(
                grad_hbm.at[:, pl.ds(0, 2 * ROWS)], grads.at[step], grad_sem.at[step]
            ).wait()

        for slot in range(4, SLABS):
            @pl.when(step == slot - 2)
            def _():
                grad_loads[slot].start()
                if slot == 6:
                    for copy in late_loads[6:]:
                        copy.start()

        @pl.when(step < SLABS)
        def _():
            part[step] = lax.dot_general(
                grads[step], attn[...], (((0,), (0,)), ((), ())), preferred_element_type=jnp.float32
            ).astype(jnp.bfloat16)
            core_copy(step).start()

        done = step - 1
        core_copy(done).wait_recv()
        rows = pl.ds(own, ROWS)
        part[done, rows, :] = part[done, rows, :] + from_core[done]

        for slot in range(1, SLABS):
            @pl.when(step == slot + 1)
            def _():
                for action in after[slot]:
                    action()

        @pl.when(jnp.logical_and(step >= first_row, step < first_row + 4))
        def _():
            attend(2 * (step - first_row))
            attend(2 * (step - first_row) + 1)

    tell(0, up_y, down_y)
    zs[0].pass_far()
    x_down(0)
    xs[0].pass_far()
    zs[1].start_far()
    x_far(1)
    zs[1].start_free()
    x_up(1)
    over_x[1][3].start()
    over_x[1][0].start()
    send_last(1)
    pl.semaphore_wait(news_sem.at[0], 2)
    tell(1, up_y, down_y)
    wait_bytes(attended.at[k, pl.ds(0, 7)], attend_sem.at[1])
    swap.start()
    pl.semaphore_wait(news_sem.at[1], 2)
    tell(2, across_x)
    weights[pl.ds(ROWS, PADDED - ROWS), :] = jnp.zeros((PADDED - ROWS, COLS), jnp.bfloat16)
    wait_bytes(state, load_sem.at[5])

    def adam(first, count, terms):
        @pl.loop(0, count // 16)
        def _(n):
            begin = pl.multiple_of(n * 16, 16)
            rows = pl.ds(pl.multiple_of(first + begin, 16), 16)
            mine = pl.ds(pl.multiple_of(own + first + begin, 16), 16)
            total = part[SLOT[0, 0], mine, :].astype(jnp.float32)
            for term in terms:
                total = total + term[pl.ds(begin, 16), :].astype(jnp.float32)
            grad = total * (1.0 / TOKENS)
            one_new = beta_one * state[1, rows, :] + (1.0 - beta_one) * grad
            two_new = beta_two * state[2, rows, :] + (1.0 - beta_two) * grad * grad
            update = (one_new * (1.0 / bias_one)) / (jnp.sqrt(two_new * (1.0 / bias_two)) + adam_eps)
            master_new = state[0, rows, :] * (1.0 - learn_rate * weight_decay) - learn_rate * update
            one_out[rows, :] = one_new
            two_out[rows, :] = two_new
            master_out[rows, :] = master_new
            weights[rows, :] = master_new.astype(jnp.bfloat16)

    def adam_x(chunk):
        xs[chunk].wait_near()
        over_x[chunk][0].wait_recv()
        _, first, count, _ = STREAMS[chunk][2]
        adam(first, count, (x_landing(chunk, 0), xs[chunk].near.at[0], xs[chunk].near.at[1]))

    def adam_z(chunk):
        zs[chunk].wait_near()
        last_x[chunk].wait_recv()
        _, first, count, _ = STREAMS[chunk][1]
        adam(first, count, (z_landing(chunk), zs[chunk].near.at[0], zs[chunk].near.at[1]))

    def product(first, count):
        halves = [
            lax.dot_general(
                attended[...].reshape(256, HALF),
                weights[pl.ds(first, count), pl.ds(HALF * half, HALF)],
                (((1,), (1,)), ((), ())),
                preferred_element_type=jnp.float32,
            ).reshape(2, 8, 16, count)[:, :, 8 * half : 8 * half + 8, :]
            for half in range(2)
        ]
        return halves[0] + halves[1]

    adam_z(0)
    adam_x(0)
    zs[1].pass_far()
    x_down(1)
    swap.wait_recv()
    share = product(0, EARLY)
    pl.semaphore_wait(news_sem.at[2], 1)
    for place in range(NZ):
        shares[place] = jnp.concatenate(
            [share[core, dx * NZ + place] for dx in range(NX) for core in range(2)], axis=0
        ).astype(jnp.bfloat16)

    for step in (2, 1, 3):
        remote(
            shares.at[lax.rem(z_summed + step, NZ)],
            arrived.at[step - 1],
            share_sem.at[0],
            share_sem.at[1],
            (f, lax.rem(y + step, 4) * 2 + x_hi),
        ).start()

    xs[1].pass_far()
    adam_z(1)
    adam_x(1)

    wait_bytes(arrived, share_sem.at[1])
    total = shares[z_summed].astype(jnp.float32)
    for step in range(3):
        total = total + arrived[step].astype(jnp.float32)
    totals[...] = total
    for dx in range(NX):
        for core in range(2):
            remote(
                totals.at[pl.ds(8 * (2 * dx + core), 8)],
                decoded.at[k, x_hi],
                share_sem.at[2],
                share_sem.at[3],
                ((dx * NZ + z_summed) * 2 + core, f // 2),
            ).start()

    late_shares[...] = product(EARLY, PADDED - EARLY).reshape(16, 8, PADDED - EARLY)

    def late_copy(step):
        target = lax.rem(f + step, 16)
        return remote(
            late_shares.at[lax.rem(target, 2) * 8 + target // 2],
            late_arrived.at[k, t],
            late_sem.at[0],
            late_sem.at[1],
            (target, f // 2),
        )

    for step in range(1, 16):
        late_copy(step).start()

    @pl.when(stays)
    def _():
        pltpu.make_async_copy(
            late_shares.at[k * 8 + f // 2], late_arrived.at[k, t], late_sem.at[1]
        ).start()

    @pl.when(jnp.logical_not(stays))
    def _():
        late_copy(0).start()

    wait_bytes(from_core, send_sem.at[0])
    wait_bytes(from_x, send_sem.at[1])
    wait_bytes(from_x_last, send_sem.at[2])
    for number, (near, far) in enumerate(((zo_near, zo_far), (zs_near, zs_far), (xs_near, xs_far))):
        wait_bytes(far, send_sem.at[3 + 2 * number])
        wait_bytes(near, send_sem.at[4 + 2 * number])
    wait_bytes(attended.at[k, pl.ds(0, 7)], attend_sem.at[0])
    swap.wait_send()
    wait_bytes(arrived, share_sem.at[0])
    wait_bytes(decoded, share_sem.at[2])

    @pl.when(stays)
    def _():
        wait_bytes(late_shares.at[pl.ds(0, 15)], late_sem.at[0])

    @pl.when(jnp.logical_not(stays))
    def _():
        wait_bytes(late_shares, late_sem.at[0])

    wait_bytes(decoded, share_sem.at[3])
    decoded_out[:, :, pl.ds(0, EARLY)] = decoded[:, 0] + decoded[:, 1]
    wait_bytes(late_arrived, late_sem.at[1])
    decoded_out[:, :, pl.ds(EARLY, PADDED - EARLY)] = jnp.sum(late_arrived[...], axis=1)


def write_kernel(master, one, two, decoded, master_out, one_out, two_out, decoded_out, rounded, sems):
    pairs = ((master, master_out), (one, one_out), (two, two_out))
    for piece in range(4):
        rows = pl.ds(ROWS // 4 * piece, ROWS // 4)
        for n, (src, dst) in enumerate(pairs):
            pltpu.make_async_copy(src.at[rows], dst.at[rows], sems.at[n]).start()
    rounded[...] = jnp.concatenate(
        [decoded[core, :, :ROWS] for core in range(2)], axis=1
    ).astype(jnp.bfloat16)
    last = pltpu.make_async_copy(rounded, decoded_out, sems.at[3])
    last.start()
    for n, (src, dst) in enumerate(pairs):
        pltpu.make_async_copy(src, dst, sems.at[n]).wait()
    last.wait()


def shards(*args):
    bf16, f32 = jnp.bfloat16, jnp.float32
    vmem = pl.BlockSpec(memory_space=pltpu.VMEM)
    anywhere = pl.BlockSpec(memory_space=pl.ANY)
    results = pl.pallas_call(
        kernel,
        out_shape=(
            pltpu.VMEM((ROWS, COLS), f32),
            pltpu.VMEM((ROWS, COLS), f32),
            pltpu.VMEM((ROWS, COLS), f32),
            pltpu.VMEM((2, 8, PADDED), f32),
        ),
        in_specs=[anywhere] * 11,
        out_specs=(vmem,) * 4,
        scratch_shapes=[
            pltpu.VMEM((1024, COLS), bf16),
            pltpu.VMEM((SLABS, 1024, 2 * ROWS), bf16),
            pltpu.VMEM((SLABS, 2 * ROWS, COLS), bf16),
            pltpu.VMEM((SLABS, ROWS, COLS), bf16),
            pltpu.VMEM((NZ, X_TOTAL, COLS), bf16),
            pltpu.VMEM((Z_TOTAL, COLS), bf16),
            pltpu.VMEM((2, Z_TOTAL, COLS), bf16),
            pltpu.VMEM((Z_TOTAL, COLS), bf16),
            pltpu.VMEM((2, Z_TOTAL, COLS), bf16),
            pltpu.VMEM((Z_TOTAL, COLS), bf16),
            pltpu.VMEM((2, X_TOTAL, COLS), bf16),
            pltpu.VMEM((X_TOTAL, COLS), bf16),
            pltpu.VMEM((3, ROWS, COLS), f32),
            pltpu.VMEM((8, 1024), bf16),
            pltpu.VMEM((8, HEAD_SIZE), bf16),
            pltpu.VMEM((8, HEAD_SIZE), bf16),
            pltpu.VMEM((2, 8, 1, CACHE_SLOTS, HEAD_SIZE), bf16),
            pltpu.SMEM((8,), jnp.int32),
            pltpu.VMEM((PADDED, COLS), bf16),
            pltpu.VMEM((64, HEAD_SIZE), f32),
            pltpu.VMEM((64, HEAD_SIZE), f32),
            pltpu.VMEM((2, 8, HEAD_SIZE), f32),
            pltpu.VMEM((2, 8, 16, HALF), bf16),
            pltpu.VMEM((NZ, 32, EARLY), bf16),
            pltpu.VMEM((3, 32, EARLY), bf16),
            pltpu.VMEM((32, EARLY), f32),
            pltpu.VMEM((2, 2, 8, EARLY), f32),
            pltpu.VMEM((16, 8, PADDED - EARLY), f32),
            pltpu.VMEM((2, 8, 8, PADDED - EARLY), f32),
            pltpu.SemaphoreType.DMA((6,)),
            pltpu.SemaphoreType.DMA((2,)),
            pltpu.SemaphoreType.DMA((SLABS,)),
            pltpu.SemaphoreType.DMA((SLABS + 1,)),
            pltpu.SemaphoreType.DMA((2, NZ + 1)),
            pltpu.SemaphoreType.DMA((2, 3, 3)),
            pltpu.SemaphoreType.DMA((4,)),
            pltpu.SemaphoreType.DMA((4,)),
            pltpu.SemaphoreType.DMA((2,)),
            pltpu.SemaphoreType.DMA((9,)),
            pltpu.SemaphoreType.REGULAR((3,)),
        ],
        compiler_params=pltpu.CompilerParams(
            collective_id=0, has_side_effects=True, vmem_limit_bytes=50 << 20
        ),
        cost_estimate=pl.CostEstimate(
            flops=2 * 1024 * 1024 * 5120, bytes_accessed=24 << 20, transcendentals=1 << 19
        ),
    )(*(pltpu.with_memory_space_constraint(arg, pltpu.HBM) for arg in args))
    return pl.pallas_call(
        write_kernel,
        out_shape=(
            jax.ShapeDtypeStruct((ROWS, COLS), f32),
            jax.ShapeDtypeStruct((ROWS, COLS), f32),
            jax.ShapeDtypeStruct((ROWS, COLS), f32),
            jax.ShapeDtypeStruct((8, 2 * ROWS), bf16),
        ),
        in_specs=[vmem] * 4,
        out_specs=(anywhere,) * 4,
        scratch_shapes=[pltpu.VMEM((8, 2 * ROWS), bf16), pltpu.SemaphoreType.DMA((4,))],
        compiler_params=pltpu.CompilerParams(vmem_limit_bytes=8 << 20),
        cost_estimate=pl.CostEstimate(flops=0, bytes_accessed=8 << 20, transcendentals=0),
    )(*results)


def solution(mesh):
    placed = (
        P("fsdp", "tp"),
        P("fsdp", None),
        P("fsdp", "tp"),
        P("fsdp", "tp"),
        P("fsdp", "tp"),
        P("fsdp", "tp"),
        P("fsdp", "tp"),
        P("fsdp", "tp"),
        P("fsdp", "tp", None, None),
        P("fsdp", "tp", None, None),
        P("fsdp"),
    )
    return jax.shard_map(
        shards,
        mesh=mesh,
        in_specs=placed,
        out_specs=(P("fsdp", "tp"), P("fsdp", "tp"), P("fsdp", "tp"), P("fsdp", "tp")),
        check_vma=False,
    )
```

```python
import jax
import jax.numpy as jnp
from jax import lax
from jax.experimental import pallas as pl
from jax.experimental.pallas import tpu as pltpu
from jax.sharding import PartitionSpec as P

MESH = pl.DeviceIdType.MESH
HEAD_SIZE = 128
CACHE_SLOTS = 1024
TOKENS = 16384

beta_one = 0.9
beta_two = 0.95
learn_rate = 0.003
weight_decay = 0.1
adam_eps = 1e-08
bias_one = 1.0 - 0.9**10
bias_two = 1.0 - 0.95**10

NX, NZ = 2, 4
ROWS = 320
COLS = 1024
HALF = COLS // 2
EARLY = 256
PADDED = 384
ORDER = ((1, 2), (1, 1), (1, 3), (0, 2), (0, 1), (0, 3), (1, 0), (0, 0))
SLABS = len(ORDER)
SLOT = {place: slot for slot, place in enumerate(ORDER)}
STREAMS = (
    ((1, 112, 144, 80), (0, 112, 144, 96), (0, 0, 112, 48)),
    ((1, 288, 32, 16), (0, 288, 32, 16), (0, 256, 32, 16)),
)
Z_TOTAL = sum(chunk[0][2] for chunk in STREAMS)
X_TOTAL = sum(chunk[2][2] for chunk in STREAMS)
Z_BEGIN = (0, STREAMS[0][0][2])
X_BEGIN = (0, STREAMS[0][2][2])


def kernel(
    attn_hbm,
    grad_hbm,
    master_hbm,
    one_hbm,
    two_hbm,
    query_hbm,
    new_key_hbm,
    new_value_hbm,
    keys_hbm,
    values_hbm,
    lengths_hbm,
    master_out,
    one_out,
    two_out,
    decoded_out,
    attn,
    grads,
    part,
    from_core,
    from_x,
    from_x_last,
    zo_near,
    zo_far,
    zs_near,
    zs_far,
    xs_near,
    xs_far,
    state,
    query,
    new_key,
    new_value,
    caches,
    lengths,
    weights,
    heads,
    mixed,
    fresh,
    attended,
    shares,
    arrived,
    totals,
    decoded,
    late_shares,
    late_arrived,
    load_sem,
    attn_sem,
    grad_sem,
    core_sem,
    x_sem,
    z_sem,
    attend_sem,
    share_sem,
    late_sem,
    send_sem,
    news_sem,
):
    f = lax.axis_index("fsdp")
    t = lax.axis_index("tp")
    x, z, k = f // (2 * NZ), lax.rem(f // 2, NZ), lax.rem(f, 2)
    y, x_hi = t // 2, lax.rem(t, 2)
    z_summed = lax.rem(z + 2 + y - f // 4 + 8, NZ)

    def chip(dx, dz):
        return lax.rem(x + dx, NX) * NZ + lax.rem(z + dz, NZ)

    def at(dx, dz, core):
        return (chip(dx, dz) * 2 + core, t)

    other_core = at(0, 0, 1 - k)
    other_x = at(1, 0, k)
    up, down = at(0, 1, k), at(0, 3, k)
    own = pl.multiple_of(k * ROWS, 64)
    given = pl.multiple_of((1 - k) * ROWS, 64)

    attn_loads = [
        pltpu.make_async_copy(
            attn_hbm.at[:, pl.ds(HALF * half, HALF)], attn.at[:, pl.ds(HALF * half, HALF)], attn_sem.at[half]
        )
        for half in range(2)
    ]
    grad_loads = []
    for slot, (dx, dz) in enumerate(ORDER):
        columns = pl.ds(pl.multiple_of(chip(dx, dz) * 2 * ROWS, 128), 2 * ROWS)
        grad_loads.append(
            pltpu.make_async_copy(grad_hbm.at[:, columns], grads.at[slot], grad_sem.at[slot])
        )
    late_loads = [
        pltpu.make_async_copy(src, dst, load_sem.at[n])
        for n, (src, dst) in enumerate(
            (
                (query_hbm, query),
                (new_key_hbm, new_key),
                (new_value_hbm, new_value),
                (lengths_hbm, lengths),
            )
        )
    ]
    late_loads += [
        pltpu.make_async_copy(keys_hbm, caches.at[0], load_sem.at[4]),
        pltpu.make_async_copy(values_hbm, caches.at[1], load_sem.at[4]),
        pltpu.make_async_copy(master_hbm, state.at[0], load_sem.at[5]),
        pltpu.make_async_copy(one_hbm, state.at[1], load_sem.at[5]),
        pltpu.make_async_copy(two_hbm, state.at[2], load_sem.at[5]),
    ]
    first_columns = pl.ds(pl.multiple_of(chip(*ORDER[0]) * 2 * ROWS, 128), 2 * ROWS)
    for piece in range(4):
        rows = pl.ds(256 * piece, 256)
        pltpu.make_async_copy(
            grad_hbm.at[rows, first_columns], grads.at[0, rows], grad_sem.at[0]
        ).start()
        pltpu.make_async_copy(
            attn_hbm.at[rows, pl.ds(0, HALF)], attn.at[rows, pl.ds(0, HALF)], attn_sem.at[0]
        ).start()

    barrier = pltpu.get_barrier_semaphore()
    up_y = (f, lax.rem(y + 1, 4) * 2 + x_hi)
    down_y = (f, lax.rem(y + 3, 4) * 2 + x_hi)
    across_x = (chip(1, 0) * 2 + k, y * 2 + 1 - x_hi)
    neighbours = (other_core, other_x, up, down, up_y, down_y, across_x)
    for device in neighbours:
        pl.semaphore_signal(barrier, inc=1, device_id=device, device_id_type=MESH)
    stays = t == f // 2

    def tell(n, *devices):
        for device in devices:
            pl.semaphore_signal(news_sem.at[n], inc=1, device_id=device, device_id_type=MESH)

    attn_loads[1].start()

    def remote(src, dst, send, recv, device):
        return pltpu.make_async_remote_copy(
            src_ref=src, dst_ref=dst, send_sem=send, recv_sem=recv, device_id=device, device_id_type=MESH
        )

    def wait_bytes(ref, sem):
        pltpu.make_async_copy(ref, ref, sem).wait()

    def core_copy(slot):
        return remote(
            part.at[slot, pl.ds(given, ROWS)],
            from_core.at[slot],
            send_sem.at[0],
            core_sem.at[slot],
            other_core,
        )

    def own_rows(dx, dz, first, count):
        rows = pl.ds(pl.multiple_of(own + first, 16), count)
        return part.at[SLOT[dx, dz], rows]

    def add_own(dx, dz, first, count, *terms):
        ref = own_rows(dx, dz, first, count)
        for begin in range(0, count, 16):
            rows = pl.ds(begin, 16)
            total = ref[rows, :]
            for term in terms:
                total = total + term[rows, :]
            ref[rows, :] = total

    def x_landing(chunk, dz):
        return from_x.at[dz, pl.ds(X_BEGIN[chunk], STREAMS[chunk][2][2])]

    def x_copy(chunk, dz):
        _, first, count, _ = STREAMS[chunk][2]
        return remote(
            own_rows(1, dz, first, count),
            x_landing(chunk, dz),
            send_sem.at[1],
            x_sem.at[chunk, dz],
            other_x,
        )

    over_x = [[x_copy(chunk, dz) for dz in range(NZ)] for chunk in range(2)]

    def z_landing(chunk):
        return from_x_last.at[pl.ds(Z_BEGIN[chunk], STREAMS[chunk][0][2])]

    def last_copy(chunk):
        _, first, count, _ = STREAMS[chunk][0]
        return remote(
            own_rows(1, 0, first, count),
            z_landing(chunk),
            send_sem.at[2],
            x_sem.at[chunk, NZ],
            other_x,
        )

    last_x = [last_copy(chunk) for chunk in range(2)]

    class Stream:
        def __init__(self, chunk, number, near, far):
            dx, first, count, cut = STREAMS[chunk][number]
            rest = count - cut
            place = pl.ds((X_BEGIN if number == 2 else Z_BEGIN)[chunk], count)
            self.dx, self.first, self.count, self.cut, self.rest = dx, first, count, cut, rest
            self.near, self.far = near.at[:, place], far.at[place]

            def send(dz, begin, size, dst, n, device):
                return remote(
                    own_rows(dx, dz, first + begin, size),
                    dst,
                    send_sem.at[3 + 2 * number + n // 2],
                    z_sem.at[chunk, number, n],
                    device,
                )

            near, far = self.near, self.far
            self.far_up = send(2, 0, cut, far.at[pl.ds(0, cut)], 0, up)
            self.far_down = send(2, cut, rest, far.at[pl.ds(cut, rest)], 1, down)
            self.up_free = send(1, cut, rest, near.at[0, pl.ds(cut, rest)], 2, up)
            self.up_late = send(1, 0, cut, near.at[0, pl.ds(0, cut)], 2, up)
            self.down_free = send(3, 0, cut, near.at[1, pl.ds(0, cut)], 2, down)
            self.down_late = send(3, cut, rest, near.at[1, pl.ds(cut, rest)], 2, down)
            self.near_sem = z_sem.at[chunk, number, 2]

        def start_far(self):
            self.far_up.start()
            self.far_down.start()

        def start_free(self):
            self.up_free.start()
            self.down_free.start()

        def pass_far(self):
            self.far_up.wait_recv()
            add_own(self.dx, 1, self.first, self.cut, self.far.at[pl.ds(0, self.cut)])
            self.up_late.start()
            self.far_down.wait_recv()
            add_own(self.dx, 3, self.first + self.cut, self.rest, self.far.at[pl.ds(self.cut, self.rest)])
            self.down_late.start()

        def wait_near(self):
            wait_bytes(self.near, self.near_sem)

    zo = [Stream(chunk, 0, zo_near, zo_far) for chunk in range(2)]
    zs = [Stream(chunk, 1, zs_near, zs_far) for chunk in range(2)]
    xs = [Stream(chunk, 2, xs_near, xs_far) for chunk in range(2)]

    def add_x(chunk, dz):
        over_x[chunk][dz].wait_recv()
        _, first, count, _ = STREAMS[chunk][2]
        add_own(0, dz, first, count, x_landing(chunk, dz))

    def x_far(chunk):
        add_x(chunk, 2)
        xs[chunk].start_far()

    def x_up(chunk):
        add_x(chunk, 1)
        xs[chunk].up_free.start()

    def x_down(chunk):
        add_x(chunk, 3)
        xs[chunk].down_free.start()

    def send_last(chunk, start=True):
        stream = zo[chunk]
        stream.wait_near()
        add_own(1, 0, stream.first, stream.count, stream.near.at[0], stream.near.at[1])
        if start:
            last_x[chunk].start()

    def split_heads():
        for copy in late_loads[:4]:
            copy.wait()
        wait_bytes(caches, load_sem.at[4])
        for head in range(8):
            heads[pl.ds(8 * head, 8), :] = query[:, pl.ds(HEAD_SIZE * head, HEAD_SIZE)].astype(jnp.float32)
        fresh[0] = new_key[...].astype(jnp.float32)
        fresh[1] = new_value[...].astype(jnp.float32)

    score_scale = 1.0 / HEAD_SIZE**0.5

    def attend(row):
        own_heads = heads[pl.ds(row, 8, stride=8), :]
        scores = (
            lax.dot_general(
                own_heads.astype(jnp.bfloat16),
                caches[0, row, 0],
                (((1,), (1,)), ((), ())),
                preferred_element_type=jnp.float32,
            )
            * score_scale
        )
        slots = lax.broadcasted_iota(jnp.int32, (8, CACHE_SLOTS), 1)
        scores = jnp.where(slots < lengths[row], scores, -jnp.inf)
        new_score = (
            jnp.sum(own_heads * fresh[0, pl.ds(row, 1), :], axis=-1, keepdims=True) * score_scale
        )
        top = jnp.maximum(jnp.max(scores, axis=-1, keepdims=True), new_score)
        expo = jnp.exp(scores - top)
        expo_new = jnp.exp(new_score - top)
        total = jnp.sum(expo, axis=-1, keepdims=True) + expo_new
        probs = (expo / total).astype(jnp.bfloat16)
        prob_new = (expo_new / total).astype(jnp.bfloat16).astype(jnp.float32)
        mixed[pl.ds(row, 8, stride=8), :] = (
            jnp.dot(probs, caches[1, row, 0], preferred_element_type=jnp.float32)
            + prob_new * fresh[1, pl.ds(row, 1), :]
        )

    here = chip(0, 0)
    gathers = [
        remote(
            attended.at[k, here],
            attended.at[k, here],
            attend_sem.at[0],
            attend_sem.at[1],
            at(place // NZ, place % NZ, k),
        )
        for place in range(1, NX * NZ)
    ]
    swap = remote(
        attended.at[k], attended.at[k], attend_sem.at[2], attend_sem.at[3], other_core
    )

    def send_attended():
        halves = [
            jnp.concatenate(
                [mixed[pl.ds(8 * head, 8), :] for head in range(4 * half, 4 * half + 4)], axis=1
            )
            for half in range(2)
        ]
        attended[k, here] = jnp.concatenate(halves, axis=0).astype(jnp.bfloat16)
        for copy in gathers:
            copy.start()

    after = (
        None,
        (over_x[0][1].start, zo[0].up_free.start, over_x[1][1].start, zo[1].up_free.start, split_heads),
        (over_x[0][3].start, zo[0].down_free.start, zo[1].down_free.start, zo[0].pass_far),
        (zs[0].start_far, zo[1].pass_far, lambda: x_far(0)),
        (zs[0].up_free.start,),
        (zs[0].down_free.start, lambda: x_up(0)),
        (lambda: send_last(0, False), send_attended, over_x[0][0].start, last_x[0].start),
        (),
    )
    first_row = 3

    def first_core_copy(half):
        columns = pl.ds(HALF * half, HALF)
        return remote(
            part.at[0, pl.ds(given, ROWS), columns],
            from_core.at[0, :, columns],
            send_sem.at[0],
            core_sem.at[SLABS * half],
            other_core,
        )

    def slab_half(slot, half, rows):
        columns = pl.ds(HALF * half, HALF)
        part[slot, rows, columns] = lax.dot_general(
            grads[slot, :, rows], attn[:, columns], (((0,), (0,)), ((), ())), preferred_element_type=jnp.float32
        ).astype(jnp.bfloat16)

    def send_first(half):
        columns = pl.ds(HALF * half, HALF)
        first_core_copy(half).wait_recv()
        for begin in range(0, ROWS, 16):
            rows = pl.ds(pl.multiple_of(own + begin, 16), 16)
            part[0, rows, columns] = part[0, rows, columns] + from_core[0, pl.ds(begin, 16), columns]
        _, first, count, _ = STREAMS[0][2]
        remote(
            own_rows(1, 2, first, count).at[:, columns],
            x_landing(0, 2).at[:, columns],
            send_sem.at[1],
            x_sem.at[0, 2],
            other_x,
        ).start()
        _, first, count, cut = STREAMS[0][0]
        for n, begin, size, device in ((0, 0, cut, up), (1, cut, count - cut, down)):
            remote(
                own_rows(1, 2, first + begin, size).at[:, columns],
                zo[0].far.at[pl.ds(begin, size), columns],
                send_sem.at[3],
                z_sem.at[0, 0, n],
                device,
            ).start()

    grad_loads[0].wait()
    for half in range(2):
        attn_loads[half].wait()
        slab_half(0, half, pl.ds(pl.multiple_of((1 - k) * 256, 128), 384))
        if half == 0:
            pl.semaphore_wait(barrier, len(neighbours))
            grad_loads[1].start()
        first_core_copy(half).start()
        slab_half(0, half, pl.ds(pl.multiple_of(k * 384, 128), 256))
    grad_loads[2].start()
    for copy in late_loads[:6]:
        copy.start()
    send_first(0)
    grad_loads[1].wait()
    slab_half(1, 0, pl.ds(0, 2 * ROWS))
    send_first(1)
    over_x[1][2].start()
    zo[1].start_far()
    slab_half(1, 1, pl.ds(0, 2 * ROWS))
    core_copy(1).start()
    grad_loads[3].start()

    @pl.loop(2, SLABS + 1)
    def _(step):
        @pl.when(step < SLABS)
        def _():
            pltpu.make_async_copy(
                grad_hbm.at[:, pl.ds(0, 2 * ROWS)], grads.at[step], grad_sem.at[step]
            ).wait()

        for slot in range(4, SLABS):
            @pl.when(step == slot - 2)
            def _():
                grad_loads[slot].start()
                if slot == 6:
                    for copy in late_loads[6:]:
                        copy.start()

        @pl.when(step < SLABS)
        def _():
            part[step] = lax.dot_general(
                grads[step], attn[...], (((0,), (0,)), ((), ())), preferred_element_type=jnp.float32
            ).astype(jnp.bfloat16)
            core_copy(step).start()

        done = step - 1
        core_copy(done).wait_recv()
        rows = pl.ds(own, ROWS)
        part[done, rows, :] = part[done, rows, :] + from_core[done]

        for slot in range(1, SLABS):
            @pl.when(step == slot + 1)
            def _():
                for action in after[slot]:
                    action()

        @pl.when(jnp.logical_and(step >= first_row, step < first_row + 4))
        def _():
            attend(2 * (step - first_row))
            attend(2 * (step - first_row) + 1)

    tell(0, up_y, down_y)
    zs[0].pass_far()
    x_down(0)
    xs[0].pass_far()
    zs[1].start_far()
    x_far(1)
    zs[1].start_free()
    x_up(1)
    over_x[1][3].start()
    over_x[1][0].start()
    send_last(1)
    pl.semaphore_wait(news_sem.at[0], 2)
    tell(1, up_y, down_y)
    wait_bytes(attended.at[k, pl.ds(0, 7)], attend_sem.at[1])
    swap.start()
    pl.semaphore_wait(news_sem.at[1], 2)
    tell(2, across_x)
    weights[pl.ds(ROWS, PADDED - ROWS), :] = jnp.zeros((PADDED - ROWS, COLS), jnp.bfloat16)
    wait_bytes(state, load_sem.at[5])

    def adam(first, count, terms):
        @pl.loop(0, count // 16)
        def _(n):
            begin = pl.multiple_of(n * 16, 16)
            rows = pl.ds(pl.multiple_of(first + begin, 16), 16)
            mine = pl.ds(pl.multiple_of(own + first + begin, 16), 16)
            total = part[SLOT[0, 0], mine, :].astype(jnp.float32)
            for term in terms:
                total = total + term[pl.ds(begin, 16), :].astype(jnp.float32)
            grad = total * (1.0 / TOKENS)
            one_new = beta_one * state[1, rows, :] + (1.0 - beta_one) * grad
            two_new = beta_two * state[2, rows, :] + (1.0 - beta_two) * grad * grad
            update = (one_new * (1.0 / bias_one)) / (jnp.sqrt(two_new * (1.0 / bias_two)) + adam_eps)
            master_new = state[0, rows, :] * (1.0 - learn_rate * weight_decay) - learn_rate * update
            one_out[rows, :] = one_new
            two_out[rows, :] = two_new
            master_out[rows, :] = master_new
            weights[rows, :] = master_new.astype(jnp.bfloat16)

    def adam_x(chunk):
        xs[chunk].wait_near()
        over_x[chunk][0].wait_recv()
        _, first, count, _ = STREAMS[chunk][2]
        adam(first, count, (x_landing(chunk, 0), xs[chunk].near.at[0], xs[chunk].near.at[1]))

    def adam_z(chunk):
        zs[chunk].wait_near()
        last_x[chunk].wait_recv()
        _, first, count, _ = STREAMS[chunk][1]
        adam(first, count, (z_landing(chunk), zs[chunk].near.at[0], zs[chunk].near.at[1]))

    def product(first, count):
        halves = [
            lax.dot_general(
                attended[...].reshape(256, HALF),
                weights[pl.ds(first, count), pl.ds(HALF * half, HALF)],
                (((1,), (1,)), ((), ())),
                preferred_element_type=jnp.float32,
            ).reshape(2, 8, 16, count)[:, :, 8 * half : 8 * half + 8, :]
            for half in range(2)
        ]
        return halves[0] + halves[1]

    adam_z(0)
    adam_x(0)
    zs[1].pass_far()
    x_down(1)
    swap.wait_recv()
    share = product(0, EARLY)
    pl.semaphore_wait(news_sem.at[2], 1)
    for place in range(NZ):
        shares[place] = jnp.concatenate(
            [share[core, dx * NZ + place] for dx in range(NX) for core in range(2)], axis=0
        ).astype(jnp.bfloat16)

    for step in (2, 1, 3):
        remote(
            shares.at[lax.rem(z_summed + step, NZ)],
            arrived.at[step - 1],
            share_sem.at[0],
            share_sem.at[1],
            (f, lax.rem(y + step, 4) * 2 + x_hi),
        ).start()

    xs[1].pass_far()
    adam_z(1)
    adam_x(1)

    wait_bytes(arrived, share_sem.at[1])
    total = shares[z_summed].astype(jnp.float32)
    for step in range(3):
        total = total + arrived[step].astype(jnp.float32)
    totals[...] = total
    for dx in range(NX):
        for core in range(2):
            remote(
                totals.at[pl.ds(8 * (2 * dx + core), 8)],
                decoded.at[k, x_hi],
                share_sem.at[2],
                share_sem.at[3],
                ((dx * NZ + z_summed) * 2 + core, f // 2),
            ).start()

    late_shares[...] = product(EARLY, PADDED - EARLY).reshape(16, 8, PADDED - EARLY)

    def late_copy(step):
        target = lax.rem(f + step, 16)
        return remote(
            late_shares.at[lax.rem(target, 2) * 8 + target // 2],
            late_arrived.at[k, t],
            late_sem.at[0],
            late_sem.at[1],
            (target, f // 2),
        )

    for step in range(1, 16):
        late_copy(step).start()

    @pl.when(stays)
    def _():
        pltpu.make_async_copy(
            late_shares.at[k * 8 + f // 2], late_arrived.at[k, t], late_sem.at[1]
        ).start()

    @pl.when(jnp.logical_not(stays))
    def _():
        late_copy(0).start()

    wait_bytes(from_core, send_sem.at[0])
    wait_bytes(from_x, send_sem.at[1])
    wait_bytes(from_x_last, send_sem.at[2])
    for number, (near, far) in enumerate(((zo_near, zo_far), (zs_near, zs_far), (xs_near, xs_far))):
        wait_bytes(far, send_sem.at[3 + 2 * number])
        wait_bytes(near, send_sem.at[4 + 2 * number])
    wait_bytes(attended.at[k, pl.ds(0, 7)], attend_sem.at[0])
    swap.wait_send()
    wait_bytes(arrived, share_sem.at[0])
    wait_bytes(decoded, share_sem.at[2])

    @pl.when(stays)
    def _():
        wait_bytes(late_shares.at[pl.ds(0, 15)], late_sem.at[0])

    @pl.when(jnp.logical_not(stays))
    def _():
        wait_bytes(late_shares, late_sem.at[0])

    wait_bytes(decoded, share_sem.at[3])
    decoded_out[:, :, pl.ds(0, EARLY)] = decoded[:, 0] + decoded[:, 1]
    wait_bytes(late_arrived, late_sem.at[1])
    decoded_out[:, :, pl.ds(EARLY, PADDED - EARLY)] = jnp.sum(late_arrived[...], axis=1)


def write_kernel(master, one, two, decoded, master_out, one_out, two_out, decoded_out, rounded, sems):
    pairs = ((master, master_out), (one, one_out), (two, two_out))
    for piece in range(4):
        rows = pl.ds(ROWS // 4 * piece, ROWS // 4)
        for n, (src, dst) in enumerate(pairs):
            pltpu.make_async_copy(src.at[rows], dst.at[rows], sems.at[n]).start()
    rounded[...] = jnp.concatenate(
        [decoded[core, :, :ROWS] for core in range(2)], axis=1
    ).astype(jnp.bfloat16)
    last = pltpu.make_async_copy(rounded, decoded_out, sems.at[3])
    last.start()
    for n, (src, dst) in enumerate(pairs):
        pltpu.make_async_copy(src, dst, sems.at[n]).wait()
    last.wait()


def shards(*args):
    bf16, f32 = jnp.bfloat16, jnp.float32
    vmem = pl.BlockSpec(memory_space=pltpu.VMEM)
    anywhere = pl.BlockSpec(memory_space=pl.ANY)
    results = pl.pallas_call(
        kernel,
        out_shape=(
            pltpu.VMEM((ROWS, COLS), f32),
            pltpu.VMEM((ROWS, COLS), f32),
            pltpu.VMEM((ROWS, COLS), f32),
            pltpu.VMEM((2, 8, PADDED), f32),
        ),
        in_specs=[anywhere] * 11,
        out_specs=(vmem,) * 4,
        scratch_shapes=[
            pltpu.VMEM((1024, COLS), bf16),
            pltpu.VMEM((SLABS, 1024, 2 * ROWS), bf16),
            pltpu.VMEM((SLABS, 2 * ROWS, COLS), bf16),
            pltpu.VMEM((SLABS, ROWS, COLS), bf16),
            pltpu.VMEM((NZ, X_TOTAL, COLS), bf16),
            pltpu.VMEM((Z_TOTAL, COLS), bf16),
            pltpu.VMEM((2, Z_TOTAL, COLS), bf16),
            pltpu.VMEM((Z_TOTAL, COLS), bf16),
            pltpu.VMEM((2, Z_TOTAL, COLS), bf16),
            pltpu.VMEM((Z_TOTAL, COLS), bf16),
            pltpu.VMEM((2, X_TOTAL, COLS), bf16),
            pltpu.VMEM((X_TOTAL, COLS), bf16),
            pltpu.VMEM((3, ROWS, COLS), f32),
            pltpu.VMEM((8, 1024), bf16),
            pltpu.VMEM((8, HEAD_SIZE), bf16),
            pltpu.VMEM((8, HEAD_SIZE), bf16),
            pltpu.VMEM((2, 8, 1, CACHE_SLOTS, HEAD_SIZE), bf16),
            pltpu.SMEM((8,), jnp.int32),
            pltpu.VMEM((PADDED, COLS), bf16),
            pltpu.VMEM((64, HEAD_SIZE), f32),
            pltpu.VMEM((64, HEAD_SIZE), f32),
            pltpu.VMEM((2, 8, HEAD_SIZE), f32),
            pltpu.VMEM((2, 8, 16, HALF), bf16),
            pltpu.VMEM((NZ, 32, EARLY), bf16),
            pltpu.VMEM((3, 32, EARLY), bf16),
            pltpu.VMEM((32, EARLY), f32),
            pltpu.VMEM((2, 2, 8, EARLY), f32),
            pltpu.VMEM((16, 8, PADDED - EARLY), f32),
            pltpu.VMEM((2, 8, 8, PADDED - EARLY), f32),
            pltpu.SemaphoreType.DMA((6,)),
            pltpu.SemaphoreType.DMA((2,)),
            pltpu.SemaphoreType.DMA((SLABS,)),
            pltpu.SemaphoreType.DMA((SLABS + 1,)),
            pltpu.SemaphoreType.DMA((2, NZ + 1)),
            pltpu.SemaphoreType.DMA((2, 3, 3)),
            pltpu.SemaphoreType.DMA((4,)),
            pltpu.SemaphoreType.DMA((4,)),
            pltpu.SemaphoreType.DMA((2,)),
            pltpu.SemaphoreType.DMA((9,)),
            pltpu.SemaphoreType.REGULAR((3,)),
        ],
        compiler_params=pltpu.CompilerParams(
            collective_id=0, has_side_effects=True, vmem_limit_bytes=50 << 20
        ),
        cost_estimate=pl.CostEstimate(
            flops=2 * 1024 * 1024 * 5120, bytes_accessed=24 << 20, transcendentals=1 << 19
        ),
    )(*(pltpu.with_memory_space_constraint(arg, pltpu.HBM) for arg in args))
    return pl.pallas_call(
        write_kernel,
        out_shape=(
            jax.ShapeDtypeStruct((ROWS, COLS), f32),
            jax.ShapeDtypeStruct((ROWS, COLS), f32),
            jax.ShapeDtypeStruct((ROWS, COLS), f32),
            jax.ShapeDtypeStruct((8, 2 * ROWS), bf16),
        ),
        in_specs=[vmem] * 4,
        out_specs=(anywhere,) * 4,
        scratch_shapes=[pltpu.VMEM((8, 2 * ROWS), bf16), pltpu.SemaphoreType.DMA((4,))],
        compiler_params=pltpu.CompilerParams(vmem_limit_bytes=8 << 20),
        cost_estimate=pl.CostEstimate(flops=0, bytes_accessed=8 << 20, transcendentals=0),
    )(*results)


def solution(mesh):
    placed = (
        P("fsdp", "tp"),
        P("fsdp", None),
        P("fsdp", "tp"),
        P("fsdp", "tp"),
        P("fsdp", "tp"),
        P("fsdp", "tp"),
        P("fsdp", "tp"),
        P("fsdp", "tp"),
        P("fsdp", "tp", None, None),
        P("fsdp", "tp", None, None),
        P("fsdp"),
    )
    return jax.shard_map(
        shards,
        mesh=mesh,
        in_specs=placed,
        out_specs=(P("fsdp", "tp"), P("fsdp", "tp"), P("fsdp", "tp"), P("fsdp", "tp")),
        check_vma=False,
    )
```

```python
import jax
import jax.numpy as jnp
from jax import lax
from jax.experimental import pallas as pl
from jax.experimental.pallas import tpu as pltpu
from jax.sharding import PartitionSpec as P

MESH = pl.DeviceIdType.MESH
HEAD_SIZE = 128
CACHE_SLOTS = 1024
TOKENS = 16384

beta_one = 0.9
beta_two = 0.95
learn_rate = 0.003
weight_decay = 0.1
adam_eps = 1e-08
bias_one = 1.0 - 0.9**10
bias_two = 1.0 - 0.95**10

NX, NZ = 2, 4
ROWS = 320
COLS = 1024
HALF = COLS // 2
EARLY = 256
PADDED = 384
ORDER = ((1, 2), (1, 1), (1, 3), (0, 2), (0, 1), (0, 3), (1, 0), (0, 0))
SLABS = len(ORDER)
SLOT = {place: slot for slot, place in enumerate(ORDER)}
STREAMS = (
    ((1, 112, 144, 80), (0, 112, 144, 96), (0, 0, 112, 48)),
    ((1, 288, 32, 16), (0, 288, 32, 16), (0, 256, 32, 16)),
)
Z_TOTAL = sum(chunk[0][2] for chunk in STREAMS)
X_TOTAL = sum(chunk[2][2] for chunk in STREAMS)
Z_BEGIN = (0, STREAMS[0][0][2])
X_BEGIN = (0, STREAMS[0][2][2])


def kernel(
    attn_hbm,
    grad_hbm,
    master_hbm,
    one_hbm,
    two_hbm,
    query_hbm,
    new_key_hbm,
    new_value_hbm,
    keys_hbm,
    values_hbm,
    lengths_hbm,
    master_out,
    one_out,
    two_out,
    decoded_out,
    attn,
    grads,
    part,
    from_core,
    from_x,
    from_x_last,
    zo_near,
    zo_far,
    zs_near,
    zs_far,
    xs_near,
    xs_far,
    state,
    query,
    new_key,
    new_value,
    caches,
    lengths,
    weights,
    heads,
    mixed,
    fresh,
    attended,
    shares,
    arrived,
    totals,
    decoded,
    late_shares,
    late_arrived,
    load_sem,
    attn_sem,
    grad_sem,
    core_sem,
    x_sem,
    z_sem,
    attend_sem,
    share_sem,
    late_sem,
    send_sem,
    news_sem,
):
    f = lax.axis_index("fsdp")
    t = lax.axis_index("tp")
    x, z, k = f // (2 * NZ), lax.rem(f // 2, NZ), lax.rem(f, 2)
    y, x_hi = t // 2, lax.rem(t, 2)
    z_summed = lax.rem(z + 2 + y - f // 4 + 8, NZ)

    def chip(dx, dz):
        return lax.rem(x + dx, NX) * NZ + lax.rem(z + dz, NZ)

    def at(dx, dz, core):
        return (chip(dx, dz) * 2 + core, t)

    other_core = at(0, 0, 1 - k)
    other_x = at(1, 0, k)
    up, down = at(0, 1, k), at(0, 3, k)
    own = pl.multiple_of(k * ROWS, 64)
    given = pl.multiple_of((1 - k) * ROWS, 64)

    attn_loads = [
        pltpu.make_async_copy(
            attn_hbm.at[:, pl.ds(HALF * half, HALF)], attn.at[:, pl.ds(HALF * half, HALF)], attn_sem.at[half]
        )
        for half in range(2)
    ]
    grad_loads = []
    for slot, (dx, dz) in enumerate(ORDER):
        columns = pl.ds(pl.multiple_of(chip(dx, dz) * 2 * ROWS, 128), 2 * ROWS)
        grad_loads.append(
            pltpu.make_async_copy(grad_hbm.at[:, columns], grads.at[slot], grad_sem.at[slot])
        )
    late_loads = [
        pltpu.make_async_copy(src, dst, load_sem.at[n])
        for n, (src, dst) in enumerate(
            (
                (query_hbm, query),
                (new_key_hbm, new_key),
                (new_value_hbm, new_value),
                (lengths_hbm, lengths),
            )
        )
    ]
    late_loads += [
        pltpu.make_async_copy(keys_hbm, caches.at[0], load_sem.at[4]),
        pltpu.make_async_copy(values_hbm, caches.at[1], load_sem.at[4]),
        pltpu.make_async_copy(master_hbm, state.at[0], load_sem.at[5]),
        pltpu.make_async_copy(one_hbm, state.at[1], load_sem.at[5]),
        pltpu.make_async_copy(two_hbm, state.at[2], load_sem.at[5]),
    ]
    first_columns = pl.ds(pl.multiple_of(chip(*ORDER[0]) * 2 * ROWS, 128), 2 * ROWS)
    for piece in range(4):
        rows = pl.ds(256 * piece, 256)
        pltpu.make_async_copy(
            grad_hbm.at[rows, first_columns], grads.at[0, rows], grad_sem.at[0]
        ).start()
        pltpu.make_async_copy(
            attn_hbm.at[rows, pl.ds(0, HALF)], attn.at[rows, pl.ds(0, HALF)], attn_sem.at[0]
        ).start()

    barrier = pltpu.get_barrier_semaphore()
    up_y = (f, lax.rem(y + 1, 4) * 2 + x_hi)
    down_y = (f, lax.rem(y + 3, 4) * 2 + x_hi)
    across_x = (chip(1, 0) * 2 + k, y * 2 + 1 - x_hi)
    neighbours = (other_core, other_x, up, down, up_y, down_y, across_x)
    for device in neighbours:
        pl.semaphore_signal(barrier, inc=1, device_id=device, device_id_type=MESH)
    stays = t == f // 2

    def tell(n, *devices):
        for device in devices:
            pl.semaphore_signal(news_sem.at[n], inc=1, device_id=device, device_id_type=MESH)

    attn_loads[1].start()

    def remote(src, dst, send, recv, device):
        return pltpu.make_async_remote_copy(
            src_ref=src, dst_ref=dst, send_sem=send, recv_sem=recv, device_id=device, device_id_type=MESH
        )

    def wait_bytes(ref, sem):
        pltpu.make_async_copy(ref, ref, sem).wait()

    def core_copy(slot):
        return remote(
            part.at[slot, pl.ds(given, ROWS)],
            from_core.at[slot],
            send_sem.at[0],
            core_sem.at[slot],
            other_core,
        )

    def own_rows(dx, dz, first, count):
        rows = pl.ds(pl.multiple_of(own + first, 16), count)
        return part.at[SLOT[dx, dz], rows]

    def add_own(dx, dz, first, count, *terms):
        ref = own_rows(dx, dz, first, count)
        for begin in range(0, count, 16):
            rows = pl.ds(begin, 16)
            total = ref[rows, :]
            for term in terms:
                total = total + term[rows, :]
            ref[rows, :] = total

    def x_landing(chunk, dz):
        return from_x.at[dz, pl.ds(X_BEGIN[chunk], STREAMS[chunk][2][2])]

    def x_copy(chunk, dz):
        _, first, count, _ = STREAMS[chunk][2]
        return remote(
            own_rows(1, dz, first, count),
            x_landing(chunk, dz),
            send_sem.at[1],
            x_sem.at[chunk, dz],
            other_x,
        )

    over_x = [[x_copy(chunk, dz) for dz in range(NZ)] for chunk in range(2)]

    def z_landing(chunk):
        return from_x_last.at[pl.ds(Z_BEGIN[chunk], STREAMS[chunk][0][2])]

    def last_copy(chunk):
        _, first, count, _ = STREAMS[chunk][0]
        return remote(
            own_rows(1, 0, first, count),
            z_landing(chunk),
            send_sem.at[2],
            x_sem.at[chunk, NZ],
            other_x,
        )

    last_x = [last_copy(chunk) for chunk in range(2)]

    class Stream:
        def __init__(self, chunk, number, near, far):
            dx, first, count, cut = STREAMS[chunk][number]
            rest = count - cut
            place = pl.ds((X_BEGIN if number == 2 else Z_BEGIN)[chunk], count)
            self.dx, self.first, self.count, self.cut, self.rest = dx, first, count, cut, rest
            self.near, self.far = near.at[:, place], far.at[place]

            def send(dz, begin, size, dst, n, device):
                return remote(
                    own_rows(dx, dz, first + begin, size),
                    dst,
                    send_sem.at[3 + 2 * number + n // 2],
                    z_sem.at[chunk, number, n],
                    device,
                )

            near, far = self.near, self.far
            self.far_up = send(2, 0, cut, far.at[pl.ds(0, cut)], 0, up)
            self.far_down = send(2, cut, rest, far.at[pl.ds(cut, rest)], 1, down)
            self.up_free = send(1, cut, rest, near.at[0, pl.ds(cut, rest)], 2, up)
            self.up_late = send(1, 0, cut, near.at[0, pl.ds(0, cut)], 2, up)
            self.down_free = send(3, 0, cut, near.at[1, pl.ds(0, cut)], 2, down)
            self.down_late = send(3, cut, rest, near.at[1, pl.ds(cut, rest)], 2, down)
            self.near_sem = z_sem.at[chunk, number, 2]

        def start_far(self):
            self.far_up.start()
            self.far_down.start()

        def start_free(self):
            self.up_free.start()
            self.down_free.start()

        def pass_far(self):
            self.far_up.wait_recv()
            add_own(self.dx, 1, self.first, self.cut, self.far.at[pl.ds(0, self.cut)])
            self.up_late.start()
            self.far_down.wait_recv()
            add_own(self.dx, 3, self.first + self.cut, self.rest, self.far.at[pl.ds(self.cut, self.rest)])
            self.down_late.start()

        def wait_near(self):
            wait_bytes(self.near, self.near_sem)

    zo = [Stream(chunk, 0, zo_near, zo_far) for chunk in range(2)]
    zs = [Stream(chunk, 1, zs_near, zs_far) for chunk in range(2)]
    xs = [Stream(chunk, 2, xs_near, xs_far) for chunk in range(2)]

    def add_x(chunk, dz):
        over_x[chunk][dz].wait_recv()
        _, first, count, _ = STREAMS[chunk][2]
        add_own(0, dz, first, count, x_landing(chunk, dz))

    def x_far(chunk):
        add_x(chunk, 2)
        xs[chunk].start_far()

    def x_up(chunk):
        add_x(chunk, 1)
        xs[chunk].up_free.start()

    def x_down(chunk):
        add_x(chunk, 3)
        xs[chunk].down_free.start()

    def send_last(chunk, start=True):
        stream = zo[chunk]
        stream.wait_near()
        add_own(1, 0, stream.first, stream.count, stream.near.at[0], stream.near.at[1])
        if start:
            last_x[chunk].start()

    def split_heads():
        for copy in late_loads[:4]:
            copy.wait()
        wait_bytes(caches, load_sem.at[4])
        for head in range(8):
            heads[pl.ds(8 * head, 8), :] = query[:, pl.ds(HEAD_SIZE * head, HEAD_SIZE)].astype(jnp.float32)
        fresh[0] = new_key[...].astype(jnp.float32)
        fresh[1] = new_value[...].astype(jnp.float32)

    score_scale = 1.0 / HEAD_SIZE**0.5

    def attend(row):
        own_heads = heads[pl.ds(row, 8, stride=8), :]
        scores = (
            lax.dot_general(
                own_heads.astype(jnp.bfloat16),
                caches[0, row, 0],
                (((1,), (1,)), ((), ())),
                preferred_element_type=jnp.float32,
            )
            * score_scale
        )
        slots = lax.broadcasted_iota(jnp.int32, (8, CACHE_SLOTS), 1)
        scores = jnp.where(slots < lengths[row], scores, -jnp.inf)
        new_score = (
            jnp.sum(own_heads * fresh[0, pl.ds(row, 1), :], axis=-1, keepdims=True) * score_scale
        )
        top = jnp.maximum(jnp.max(scores, axis=-1, keepdims=True), new_score)
        expo = jnp.exp(scores - top)
        expo_new = jnp.exp(new_score - top)
        total = jnp.sum(expo, axis=-1, keepdims=True) + expo_new
        probs = (expo / total).astype(jnp.bfloat16)
        prob_new = (expo_new / total).astype(jnp.bfloat16).astype(jnp.float32)
        mixed[pl.ds(row, 8, stride=8), :] = (
            jnp.dot(probs, caches[1, row, 0], preferred_element_type=jnp.float32)
            + prob_new * fresh[1, pl.ds(row, 1), :]
        )

    here = chip(0, 0)
    gathers = [
        remote(
            attended.at[k, here],
            attended.at[k, here],
            attend_sem.at[0],
            attend_sem.at[1],
            at(place // NZ, place % NZ, k),
        )
        for place in range(1, NX * NZ)
    ]
    swap = remote(
        attended.at[k], attended.at[k], attend_sem.at[2], attend_sem.at[3], other_core
    )

    def send_attended():
        halves = [
            jnp.concatenate(
                [mixed[pl.ds(8 * head, 8), :] for head in range(4 * half, 4 * half + 4)], axis=1
            )
            for half in range(2)
        ]
        attended[k, here] = jnp.concatenate(halves, axis=0).astype(jnp.bfloat16)
        for copy in gathers:
            copy.start()

    after = (
        None,
        (over_x[0][1].start, zo[0].up_free.start, over_x[1][1].start, zo[1].up_free.start, split_heads),
        (over_x[0][3].start, zo[0].down_free.start, zo[1].down_free.start, zo[0].pass_far),
        (zs[0].start_far, zo[1].pass_far, lambda: x_far(0)),
        (zs[0].up_free.start,),
        (zs[0].down_free.start, lambda: x_up(0)),
        (lambda: send_last(0, False), send_attended, over_x[0][0].start, last_x[0].start),
        (),
    )
    first_row = 3

    def first_core_copy(half):
        columns = pl.ds(HALF * half, HALF)
        return remote(
            part.at[0, pl.ds(given, ROWS), columns],
            from_core.at[0, :, columns],
            send_sem.at[0],
            core_sem.at[SLABS * half],
            other_core,
        )

    def slab_half(slot, half, rows):
        columns = pl.ds(HALF * half, HALF)
        part[slot, rows, columns] = lax.dot_general(
            grads[slot, :, rows], attn[:, columns], (((0,), (0,)), ((), ())), preferred_element_type=jnp.float32
        ).astype(jnp.bfloat16)

    def send_first(half):
        columns = pl.ds(HALF * half, HALF)
        first_core_copy(half).wait_recv()
        for begin in range(0, ROWS, 16):
            rows = pl.ds(pl.multiple_of(own + begin, 16), 16)
            part[0, rows, columns] = part[0, rows, columns] + from_core[0, pl.ds(begin, 16), columns]
        _, first, count, _ = STREAMS[0][2]
        remote(
            own_rows(1, 2, first, count).at[:, columns],
            x_landing(0, 2).at[:, columns],
            send_sem.at[1],
            x_sem.at[0, 2],
            other_x,
        ).start()
        _, first, count, cut = STREAMS[0][0]
        for n, begin, size, device in ((0, 0, cut, up), (1, cut, count - cut, down)):
            remote(
                own_rows(1, 2, first + begin, size).at[:, columns],
                zo[0].far.at[pl.ds(begin, size), columns],
                send_sem.at[3],
                z_sem.at[0, 0, n],
                device,
            ).start()

    grad_loads[0].wait()
    for half in range(2):
        attn_loads[half].wait()
        slab_half(0, half, pl.ds(pl.multiple_of((1 - k) * 256, 128), 384))
        if half == 0:
            pl.semaphore_wait(barrier, len(neighbours))
            grad_loads[1].start()
        first_core_copy(half).start()
        slab_half(0, half, pl.ds(pl.multiple_of(k * 384, 128), 256))
    grad_loads[2].start()
    for copy in late_loads[:6]:
        copy.start()
    send_first(0)
    grad_loads[1].wait()
    slab_half(1, 0, pl.ds(0, 2 * ROWS))
    send_first(1)
    over_x[1][2].start()
    zo[1].start_far()
    slab_half(1, 1, pl.ds(0, 2 * ROWS))
    core_copy(1).start()
    grad_loads[3].start()

    @pl.loop(2, SLABS + 1)
    def _(step):
        @pl.when(step < SLABS)
        def _():
            pltpu.make_async_copy(
                grad_hbm.at[:, pl.ds(0, 2 * ROWS)], grads.at[step], grad_sem.at[step]
            ).wait()

        for slot in range(4, SLABS):
            @pl.when(step == slot - 2)
            def _():
                grad_loads[slot].start()
                if slot == 6:
                    for copy in late_loads[6:]:
                        copy.start()

        @pl.when(step < SLABS)
        def _():
            part[step] = lax.dot_general(
                grads[step], attn[...], (((0,), (0,)), ((), ())), preferred_element_type=jnp.float32
            ).astype(jnp.bfloat16)
            core_copy(step).start()

        done = step - 1
        core_copy(done).wait_recv()
        rows = pl.ds(own, ROWS)
        part[done, rows, :] = part[done, rows, :] + from_core[done]

        for slot in range(1, SLABS):
            @pl.when(step == slot + 1)
            def _():
                for action in after[slot]:
                    action()

        @pl.when(jnp.logical_and(step >= first_row, step < first_row + 4))
        def _():
            attend(2 * (step - first_row))
            attend(2 * (step - first_row) + 1)

    tell(0, up_y, down_y)
    zs[0].pass_far()
    x_down(0)
    xs[0].pass_far()
    zs[1].start_far()
    x_far(1)
    zs[1].start_free()
    x_up(1)
    over_x[1][3].start()
    over_x[1][0].start()
    send_last(1)
    pl.semaphore_wait(news_sem.at[0], 2)
    tell(1, up_y, down_y)
    wait_bytes(attended.at[k, pl.ds(0, 7)], attend_sem.at[1])
    swap.start()
    pl.semaphore_wait(news_sem.at[1], 2)
    tell(2, across_x)
    weights[pl.ds(ROWS, PADDED - ROWS), :] = jnp.zeros((PADDED - ROWS, COLS), jnp.bfloat16)
    wait_bytes(state, load_sem.at[5])

    def adam(first, count, terms):
        @pl.loop(0, count // 16)
        def _(n):
            begin = pl.multiple_of(n * 16, 16)
            rows = pl.ds(pl.multiple_of(first + begin, 16), 16)
            mine = pl.ds(pl.multiple_of(own + first + begin, 16), 16)
            total = part[SLOT[0, 0], mine, :].astype(jnp.float32)
            for term in terms:
                total = total + term[pl.ds(begin, 16), :].astype(jnp.float32)
            grad = total * (1.0 / TOKENS)
            one_new = beta_one * state[1, rows, :] + (1.0 - beta_one) * grad
            two_new = beta_two * state[2, rows, :] + (1.0 - beta_two) * grad * grad
            update = (one_new * (1.0 / bias_one)) / (jnp.sqrt(two_new * (1.0 / bias_two)) + adam_eps)
            master_new = state[0, rows, :] * (1.0 - learn_rate * weight_decay) - learn_rate * update
            one_out[rows, :] = one_new
            two_out[rows, :] = two_new
            master_out[rows, :] = master_new
            weights[rows, :] = master_new.astype(jnp.bfloat16)

    def adam_x(chunk):
        xs[chunk].wait_near()
        over_x[chunk][0].wait_recv()
        _, first, count, _ = STREAMS[chunk][2]
        adam(first, count, (x_landing(chunk, 0), xs[chunk].near.at[0], xs[chunk].near.at[1]))

    def adam_z(chunk):
        zs[chunk].wait_near()
        last_x[chunk].wait_recv()
        _, first, count, _ = STREAMS[chunk][1]
        adam(first, count, (z_landing(chunk), zs[chunk].near.at[0], zs[chunk].near.at[1]))

    def product(first, count):
        halves = [
            lax.dot_general(
                attended[...].reshape(256, HALF),
                weights[pl.ds(first, count), pl.ds(HALF * half, HALF)],
                (((1,), (1,)), ((), ())),
                preferred_element_type=jnp.float32,
            ).reshape(2, 8, 16, count)[:, :, 8 * half : 8 * half + 8, :]
            for half in range(2)
        ]
        return halves[0] + halves[1]

    adam_z(0)
    adam_x(0)
    zs[1].pass_far()
    x_down(1)
    swap.wait_recv()
    share = product(0, EARLY)
    pl.semaphore_wait(news_sem.at[2], 1)
    for place in range(NZ):
        shares[place] = jnp.concatenate(
            [share[core, dx * NZ + place] for dx in range(NX) for core in range(2)], axis=0
        ).astype(jnp.bfloat16)

    for step in (2, 1, 3):
        remote(
            shares.at[lax.rem(z_summed + step, NZ)],
            arrived.at[step - 1],
            share_sem.at[0],
            share_sem.at[1],
            (f, lax.rem(y + step, 4) * 2 + x_hi),
        ).start()

    xs[1].pass_far()
    adam_z(1)
    adam_x(1)

    wait_bytes(arrived, share_sem.at[1])
    total = shares[z_summed].astype(jnp.float32)
    for step in range(3):
        total = total + arrived[step].astype(jnp.float32)
    totals[...] = total
    for dx in range(NX):
        for core in range(2):
            remote(
                totals.at[pl.ds(8 * (2 * dx + core), 8)],
                decoded.at[k, x_hi],
                share_sem.at[2],
                share_sem.at[3],
                ((dx * NZ + z_summed) * 2 + core, f // 2),
            ).start()

    late_shares[...] = product(EARLY, PADDED - EARLY).reshape(16, 8, PADDED - EARLY)

    def late_copy(dx, dz, core):
        target = chip(dx, dz) * 2 + lax.rem(k + core, 2)
        return remote(
            late_shares.at[lax.rem(target, 2) * 8 + target // 2],
            late_arrived.at[k, t],
            late_sem.at[0],
            late_sem.at[1],
            (target, f // 2),
        )

    places = [(dx, dz, core) for dz in (2, 1, 3, 0) for dx in (1, 0) for core in (1, 0)]
    for place in places[:-1]:
        late_copy(*place).start()

    @pl.when(stays)
    def _():
        pltpu.make_async_copy(
            late_shares.at[k * 8 + f // 2], late_arrived.at[k, t], late_sem.at[1]
        ).start()

    @pl.when(jnp.logical_not(stays))
    def _():
        late_copy(*places[-1]).start()

    wait_bytes(from_core, send_sem.at[0])
    wait_bytes(from_x, send_sem.at[1])
    wait_bytes(from_x_last, send_sem.at[2])
    for number, (near, far) in enumerate(((zo_near, zo_far), (zs_near, zs_far), (xs_near, xs_far))):
        wait_bytes(far, send_sem.at[3 + 2 * number])
        wait_bytes(near, send_sem.at[4 + 2 * number])
    wait_bytes(attended.at[k, pl.ds(0, 7)], attend_sem.at[0])
    swap.wait_send()
    wait_bytes(arrived, share_sem.at[0])
    wait_bytes(decoded, share_sem.at[2])

    @pl.when(stays)
    def _():
        wait_bytes(late_shares.at[pl.ds(0, 15)], late_sem.at[0])

    @pl.when(jnp.logical_not(stays))
    def _():
        wait_bytes(late_shares, late_sem.at[0])

    wait_bytes(decoded, share_sem.at[3])
    decoded_out[:, :, pl.ds(0, EARLY)] = decoded[:, 0] + decoded[:, 1]
    wait_bytes(late_arrived, late_sem.at[1])
    decoded_out[:, :, pl.ds(EARLY, PADDED - EARLY)] = jnp.sum(late_arrived[...], axis=1)


def write_kernel(master, one, two, decoded, master_out, one_out, two_out, decoded_out, rounded, sems):
    pairs = ((master, master_out), (one, one_out), (two, two_out))
    for piece in range(4):
        rows = pl.ds(ROWS // 4 * piece, ROWS // 4)
        for n, (src, dst) in enumerate(pairs):
            pltpu.make_async_copy(src.at[rows], dst.at[rows], sems.at[n]).start()
    rounded[...] = jnp.concatenate(
        [decoded[core, :, :ROWS] for core in range(2)], axis=1
    ).astype(jnp.bfloat16)
    last = pltpu.make_async_copy(rounded, decoded_out, sems.at[3])
    last.start()
    for n, (src, dst) in enumerate(pairs):
        pltpu.make_async_copy(src, dst, sems.at[n]).wait()
    last.wait()


def shards(*args):
    bf16, f32 = jnp.bfloat16, jnp.float32
    vmem = pl.BlockSpec(memory_space=pltpu.VMEM)
    anywhere = pl.BlockSpec(memory_space=pl.ANY)
    results = pl.pallas_call(
        kernel,
        out_shape=(
            pltpu.VMEM((ROWS, COLS), f32),
            pltpu.VMEM((ROWS, COLS), f32),
            pltpu.VMEM((ROWS, COLS), f32),
            pltpu.VMEM((2, 8, PADDED), f32),
        ),
        in_specs=[anywhere] * 11,
        out_specs=(vmem,) * 4,
        scratch_shapes=[
            pltpu.VMEM((1024, COLS), bf16),
            pltpu.VMEM((SLABS, 1024, 2 * ROWS), bf16),
            pltpu.VMEM((SLABS, 2 * ROWS, COLS), bf16),
            pltpu.VMEM((SLABS, ROWS, COLS), bf16),
            pltpu.VMEM((NZ, X_TOTAL, COLS), bf16),
            pltpu.VMEM((Z_TOTAL, COLS), bf16),
            pltpu.VMEM((2, Z_TOTAL, COLS), bf16),
            pltpu.VMEM((Z_TOTAL, COLS), bf16),
            pltpu.VMEM((2, Z_TOTAL, COLS), bf16),
            pltpu.VMEM((Z_TOTAL, COLS), bf16),
            pltpu.VMEM((2, X_TOTAL, COLS), bf16),
            pltpu.VMEM((X_TOTAL, COLS), bf16),
            pltpu.VMEM((3, ROWS, COLS), f32),
            pltpu.VMEM((8, 1024), bf16),
            pltpu.VMEM((8, HEAD_SIZE), bf16),
            pltpu.VMEM((8, HEAD_SIZE), bf16),
            pltpu.VMEM((2, 8, 1, CACHE_SLOTS, HEAD_SIZE), bf16),
            pltpu.SMEM((8,), jnp.int32),
            pltpu.VMEM((PADDED, COLS), bf16),
            pltpu.VMEM((64, HEAD_SIZE), f32),
            pltpu.VMEM((64, HEAD_SIZE), f32),
            pltpu.VMEM((2, 8, HEAD_SIZE), f32),
            pltpu.VMEM((2, 8, 16, HALF), bf16),
            pltpu.VMEM((NZ, 32, EARLY), bf16),
            pltpu.VMEM((3, 32, EARLY), bf16),
            pltpu.VMEM((32, EARLY), f32),
            pltpu.VMEM((2, 2, 8, EARLY), f32),
            pltpu.VMEM((16, 8, PADDED - EARLY), f32),
            pltpu.VMEM((2, 8, 8, PADDED - EARLY), f32),
            pltpu.SemaphoreType.DMA((6,)),
            pltpu.SemaphoreType.DMA((2,)),
            pltpu.SemaphoreType.DMA((SLABS,)),
            pltpu.SemaphoreType.DMA((SLABS + 1,)),
            pltpu.SemaphoreType.DMA((2, NZ + 1)),
            pltpu.SemaphoreType.DMA((2, 3, 3)),
            pltpu.SemaphoreType.DMA((4,)),
            pltpu.SemaphoreType.DMA((4,)),
            pltpu.SemaphoreType.DMA((2,)),
            pltpu.SemaphoreType.DMA((9,)),
            pltpu.SemaphoreType.REGULAR((3,)),
        ],
        compiler_params=pltpu.CompilerParams(
            collective_id=0, has_side_effects=True, vmem_limit_bytes=50 << 20
        ),
        cost_estimate=pl.CostEstimate(
            flops=2 * 1024 * 1024 * 5120, bytes_accessed=24 << 20, transcendentals=1 << 19
        ),
    )(*(pltpu.with_memory_space_constraint(arg, pltpu.HBM) for arg in args))
    return pl.pallas_call(
        write_kernel,
        out_shape=(
            jax.ShapeDtypeStruct((ROWS, COLS), f32),
            jax.ShapeDtypeStruct((ROWS, COLS), f32),
            jax.ShapeDtypeStruct((ROWS, COLS), f32),
            jax.ShapeDtypeStruct((8, 2 * ROWS), bf16),
        ),
        in_specs=[vmem] * 4,
        out_specs=(anywhere,) * 4,
        scratch_shapes=[pltpu.VMEM((8, 2 * ROWS), bf16), pltpu.SemaphoreType.DMA((4,))],
        compiler_params=pltpu.CompilerParams(vmem_limit_bytes=8 << 20),
        cost_estimate=pl.CostEstimate(flops=0, bytes_accessed=8 << 20, transcendentals=0),
    )(*results)


def solution(mesh):
    placed = (
        P("fsdp", "tp"),
        P("fsdp", None),
        P("fsdp", "tp"),
        P("fsdp", "tp"),
        P("fsdp", "tp"),
        P("fsdp", "tp"),
        P("fsdp", "tp"),
        P("fsdp", "tp"),
        P("fsdp", "tp", None, None),
        P("fsdp", "tp", None, None),
        P("fsdp"),
    )
    return jax.shard_map(
        shards,
        mesh=mesh,
        in_specs=placed,
        out_specs=(P("fsdp", "tp"), P("fsdp", "tp"), P("fsdp", "tp"), P("fsdp", "tp")),
        check_vma=False,
    )
```
